256 devices in a mesh: gx: 32 (over z_hi, x, y), gy: 8 (over z_lo, core).
Axes of the slice: x: 4, y: 4, z: 8 (z_hi: 2, z_lo: 4; z = z_hi * 4 + z_lo), core: 2. Of those that a mesh axis runs over, the one named last changes fastest.
Arguments:
- populations: float32 [27, 24, 256, 1024], P(None, None, 'gx', 'gy'), may hold values from 0 to 1, as said below
- solid_mask: int32 [24, 256, 1024], P(None, 'gx', 'gy'), may hold values from 0 to 1, as said below
- link_cell: int32 [1048576], P(('gx', 'gy')), may hold values from 0 to 24575, as said below
- link_dir: int32 [1048576], P(('gx', 'gy')), may hold values from 0 to 26, as said below
- link_second: int32 [1048576], P(('gx', 'gy')), may hold values from 0 to 31199, as said below
- link_q: float32 [1048576], P(('gx', 'gy')), may hold values from 0.05 to 0.95
- link_panel: int32 [1048576], P(('gx', 'gy')), may hold values from -1 to 32767, as said below
Outputs:
- populations_next: float32 [27, 24, 256, 1024], P(None, None, 'gx', 'gy')
- panel_force: float32 [3, 32768], P(None, ('gx', 'gy'))
The draws below stay inside these ranges and needn't reach their ends.
Inputs may be any that keep to these rules, and one draw needn't show every extreme that they name: `solid_mask`: every value is 0 or 1; building cells stand in columns of 2 x 2 cells rising from the ground. `populations`: positive; the cell's populations are near a discrete equilibrium with density near 1 and speed under 0.25. `link_cell`: within one tile the live slots come first and name distinct cells. `link_dir`: never 13 (the rest direction); the second node lies inside 0..23 vertically. `link_second`: it is the link's cell minus c_d, widened coordinates. `link_panel`: panel p is owned by tile p // 128, tiles numbered streamwise index times 8 plus spanwise index; a live link's panel is owned by its own tile or by the tile one step streamwise before or after it (periodic) with the same spanwise index. In every draw one tile has all 4096 slots live and another has 512.
All inputs are finite; a program needn't handle non-finite values.
Results may differ from the reference program's by a relative error of at most 0.0003.
Values sent between devices are 32-bit elements; how exact they have to be, the bound alone decides.
No kernel may reach another device: no remote copies, remote signals or barrier semaphores. Data moves between devices by JAX's collectives and lax.ppermute only.
A program may use at most 128 MiB of HBM per device.

```python
import jax
import jax.numpy as jnp
from jax import lax

CX = 8
CY = 128
Z = 24
LINKS_DEV = 4096
PAN_DEV = 128
NX = 256
NY = 1024
LINKS = 1048576
PANELS = 32768
N_GX = 32
N_GY = 8


def link_tables(key):
    tile_count = N_GX * N_GY
    cell_count = Z * CX * CY
    keys = jax.random.split(key, 6)
    chosen = jax.vmap(lambda single: jax.random.permutation(single, cell_count)[:LINKS_DEV])(jax.random.split(keys[0], tile_count)).astype(jnp.int32)
    direction = jax.random.randint(keys[1], (tile_count, LINKS_DEV), 0, 26)
    direction = direction + (direction >= 13).astype(jnp.int32)
    cell_z = chosen // (CX * CY)
    cell_x = chosen // CY % CX
    cell_y = chosen % CY
    lift = direction % 3 - 1
    outside = (cell_z - lift < 0) | (cell_z - lift >= Z)
    direction = jnp.where(outside, direction - 2 * lift, direction)
    lift = direction % 3 - 1
    step_x = direction // 9 - 1
    step_y = direction // 3 % 3 - 1
    second = (cell_z - lift) * ((CX + 2) * (CY + 2)) + (cell_x - step_x + 1) * (CY + 2) + (cell_y - step_y + 1)
    counts = jax.random.randint(keys[2], (tile_count,), LINKS_DEV // 8, LINKS_DEV + 1)
    busiest = jax.random.randint(keys[3], (), 0, tile_count)
    tiles = jnp.arange(tile_count, dtype=jnp.int32)
    counts = jnp.where(tiles == busiest, LINKS_DEV, counts)
    counts = jnp.where(tiles == (busiest + 1) % tile_count, LINKS_DEV // 8, counts)
    active = jnp.arange(LINKS_DEV, dtype=jnp.int32)[None, :] < counts[:, None]
    tile_x = tiles // N_GY
    tile_y = tiles % N_GY
    stride = jax.random.randint(keys[4], (tile_count, LINKS_DEV), -1, 2)
    owner_tile = (tile_x[:, None] + stride) % N_GX * N_GY + tile_y[:, None]
    panel_id = owner_tile * PAN_DEV + jax.random.randint(keys[5], (tile_count, LINKS_DEV), 0, PAN_DEV)
    panel_id = jnp.where(active, panel_id, -1)
    return (chosen.reshape(-1), direction.reshape(-1), second.reshape(-1), panel_id.reshape(-1))


def draw_link_cell(key, part):
    tables = link_tables(key)
    return tables[0]


def draw_link_dir(key, part):
    tables = link_tables(key)
    return tables[1]


def draw_link_second(key, part):
    tables = link_tables(key)
    return tables[2]


def draw_link_panel(key, part):
    tables = link_tables(key)
    return tables[3]


def draw_solid_mask(key, part):
    key = jax.random.fold_in(key, 5)
    keys = jax.random.split(key, 2)
    footprint = jax.random.randint(keys[0], (NX // 2, NY // 2), 0, 4) == 0
    height = jax.random.randint(keys[1], (NX // 2, NY // 2), 1, Z + 1)
    footprint = jnp.repeat(jnp.repeat(footprint, 2, 0), 2, 1)
    height = jnp.repeat(jnp.repeat(height, 2, 0), 2, 1)
    levels = jnp.arange(Z, dtype=jnp.int32)[:, None, None]
    return ((levels < height[None]) & footprint[None]).astype(jnp.int32)


def draw_populations(key, part):
    key = jax.random.fold_in(key, 6)
    keys = jax.random.split(key, 3)
    grid_shape = (Z, NX, NY)
    density = jax.random.uniform(keys[0], grid_shape, jnp.float32, 0.9, 1.1)
    velocity = 0.08 * jax.random.truncated_normal(keys[1], -1.5, 1.5, (3,) + grid_shape, jnp.float32)
    jitter = 0.1 * jax.random.truncated_normal(keys[2], -2.5, 2.5, (27,) + grid_shape, jnp.float32)
    square = velocity[0] * velocity[0] + velocity[1] * velocity[1] + velocity[2] * velocity[2]
    fields = []
    for direction in range(27):
        steps = [direction // 9 - 1, direction // 3 % 3 - 1, direction % 3 - 1]
        moving = abs(steps[0]) + abs(steps[1]) + abs(steps[2])
        weight = [8.0 / 27.0, 2.0 / 27.0, 1.0 / 54.0, 1.0 / 216.0][moving]
        along = steps[0] * velocity[0] + steps[1] * velocity[1] + steps[2] * velocity[2]
        balance = weight * density * (1.0 + 3.0 * along + 4.5 * along * along - 1.5 * square)
        fields.append(balance * (1.0 + jitter[direction]))
    return jnp.stack(fields).astype(jnp.float32)


def steps_of(own_key, extent, shards, low, high):
    def one(dim, parts):
        draws = jax.random.uniform(jax.random.fold_in(jax.random.fold_in(own_key, 6), dim), (parts,), jnp.float32, low / len(shards), high / len(shards))
        return jnp.repeat(jnp.exp(draws), extent[dim] // parts).reshape((-1,) + (1,) * (len(extent) - dim - 1))

    level = one(*shards[0])
    for cut in shards[1:]:
        level = level * one(*cut)
    return level


def setup_inputs(seed: int = 0) -> dict:
    key_of = jax.random.split(jax.random.key(seed), 8)
    populations = draw_populations(jax.random.fold_in(key_of[7], 71), 0)
    solid_mask = draw_solid_mask(jax.random.fold_in(key_of[7], 71), 0)
    link_cell = draw_link_cell(jax.random.fold_in(key_of[7], 71), 0)
    link_dir = draw_link_dir(jax.random.fold_in(key_of[7], 71), 0)
    link_second = draw_link_second(jax.random.fold_in(key_of[7], 71), 0)
    link_q = jnp.clip(0.05 + 0.9 * jax.random.uniform(key_of[5], (LINKS,), jnp.float32) ** steps_of(key_of[5], (LINKS,), ((0, 256),), -0.2, 0.2), 0.05, 0.95)
    link_panel = draw_link_panel(jax.random.fold_in(key_of[7], 71), 0)
    return {"populations": populations, "solid_mask": solid_mask, "link_cell": link_cell, "link_dir": link_dir, "link_second": link_second, "link_q": link_q, "link_panel": link_panel}


RELAXATION = 1.7


def mixed_sum(plane_sum):
    return plane_sum[2, 2] + plane_sum[0, 0] - plane_sum[2, 0] - plane_sum[0, 2]


def raw_moments(populations):
    lattice = populations.reshape((3, 3, 3) + populations.shape[1:])
    along_x = lattice.sum((1, 2))
    along_y = lattice.sum((0, 2))
    along_z = lattice.sum((0, 1))
    density = along_x.sum(0)
    return jnp.stack([density, along_x[2] - along_x[0], along_y[2] - along_y[0], along_z[2] - along_z[0],
                      along_x[2] + along_x[0], along_y[2] + along_y[0], along_z[2] + along_z[0],
                      mixed_sum(lattice.sum(2)), mixed_sum(lattice.sum(1)), mixed_sum(lattice.sum(0))])


def inverse_basis(velocity):
    square = velocity * velocity
    return [[(square - velocity) / 2.0, (2.0 * velocity - 1.0) / 2.0, 0.5],
            [1.0 - square, -2.0 * velocity, -1.0],
            [(square + velocity) / 2.0, (2.0 * velocity + 1.0) / 2.0, 0.5]]


def place_key(first, second_index, inserted, axis):
    if axis == 0:
        return (inserted, first, second_index)
    if axis == 1:
        return (first, inserted, second_index)
    return (first, second_index, inserted)


def apply_axis(entries, velocity, axis):
    weights = inverse_basis(velocity)
    result = {}
    for first in range(3):
        for second_index in range(3):
            for target in range(3):
                summed = None
                for power in range(3):
                    source = place_key(first, second_index, power, axis)
                    if source in entries:
                        term = weights[target][power] * entries[source]
                        summed = term if summed is None else summed + term
                if summed is not None:
                    result[place_key(first, second_index, target, axis)] = summed
    return result


def relax(moments):
    density = moments[0]
    velocity = [moments[1] / density, moments[2] / density, moments[3] / density]

    def spread_of(row, first, second_index, diagonal):
        central = moments[row] / density - velocity[first] * velocity[second_index]
        return (1.0 - RELAXATION) * central + (RELAXATION / 3.0) * diagonal

    var_xx = spread_of(4, 0, 0, 1.0)
    var_yy = spread_of(5, 1, 1, 1.0)
    var_zz = spread_of(6, 2, 2, 1.0)
    var_xy = spread_of(7, 0, 1, 0.0)
    var_xz = spread_of(8, 0, 2, 0.0)
    var_yz = spread_of(9, 1, 2, 0.0)
    entries = {(0, 0, 0): jnp.ones_like(density), (2, 0, 0): var_xx, (0, 2, 0): var_yy, (0, 0, 2): var_zz,
               (1, 1, 0): var_xy, (1, 0, 1): var_xz, (0, 1, 1): var_yz,
               (2, 2, 0): var_xx * var_yy + 2.0 * var_xy * var_xy,
               (2, 0, 2): var_xx * var_zz + 2.0 * var_xz * var_xz,
               (0, 2, 2): var_yy * var_zz + 2.0 * var_yz * var_yz,
               (2, 1, 1): var_xx * var_yz + 2.0 * var_xy * var_xz,
               (1, 2, 1): var_yy * var_xz + 2.0 * var_xy * var_yz,
               (1, 1, 2): var_zz * var_xy + 2.0 * var_xz * var_yz,
               (2, 2, 2): var_xx * var_yy * var_zz + 2.0 * (var_xx * var_yz * var_yz + var_yy * var_xz * var_xz
                                                           + var_zz * var_xy * var_xy) + 8.0 * var_xy * var_yz * var_xz}
    sectioned = apply_axis(entries, velocity[2], 2)
    sectioned = apply_axis(sectioned, velocity[1], 1)
    sectioned = apply_axis(sectioned, velocity[0], 0)
    return jnp.stack([density * sectioned[(a, b, c)] for a in range(3) for b in range(3) for c in range(3)])


def wall_shift(shifted, reverse, lift):
    if lift == 1:
        return jnp.concatenate([reverse[:1], shifted[:-1]], 0)
    if lift == -1:
        return jnp.concatenate([shifted[1:], reverse[-1:]], 0)
    return shifted


def interpolate(fraction, toward, second, reverse):
    near = 2.0 * fraction * toward + (1.0 - 2.0 * fraction) * second
    far = toward / (2.0 * fraction) + (2.0 * fraction - 1.0) / (2.0 * fraction) * reverse
    return jnp.where(fraction < 0.5, near, far)


def reference(populations, solid_mask, link_cell, link_dir, link_second, link_q, link_panel):
    def collide_slab(index):
        slab = lax.dynamic_slice_in_dim(populations, index * CX, CX, 2)
        return relax(raw_moments(slab))

    slabs = lax.map(collide_slab, jnp.arange(N_GX, dtype=jnp.int32))
    collided = jnp.moveaxis(slabs, 0, 2).reshape(27, Z, NX, NY)
    fields = []
    for direction in range(27):
        step_x = direction // 9 - 1
        step_y = (direction // 3) % 3 - 1
        step_z = direction % 3 - 1
        shifted = jnp.roll(collided[direction], (step_x, step_y), (1, 2))
        fields.append(wall_shift(shifted, collided[26 - direction], step_z))
    cell_count = Z * NX * NY
    flat_new = jnp.stack(fields).reshape(27 * cell_count)
    flat_post = collided.reshape(27 * cell_count)
    tile_of = jnp.arange(LINKS, dtype=jnp.int32) // LINKS_DEV
    tile_x = tile_of // N_GY
    tile_y = tile_of % N_GY
    cell_z = link_cell // (CX * CY)
    cell_x = (link_cell // CY) % CX
    cell_y = link_cell % CY
    global_cell = cell_z * (NX * NY) + (tile_x * CX + cell_x) * NY + tile_y * CY + cell_y
    wide = (CX + 2) * (CY + 2)
    second_z = link_second // wide
    second_x = (link_second // (CY + 2)) % (CX + 2)
    second_y = link_second % (CY + 2)
    global_second = second_z * (NX * NY) + ((tile_x * CX + second_x - 1) % NX) * NY + (tile_y * CY + second_y - 1) % NY
    active = link_panel >= 0
    toward = flat_post[link_dir * cell_count + global_cell]
    second = flat_post[link_dir * cell_count + global_second]
    reverse = flat_post[(26 - link_dir) * cell_count + global_cell]
    bounce = interpolate(link_q, toward, second, reverse)
    target = (26 - link_dir) * cell_count + global_cell
    flat_new = flat_new.at[target].set(jnp.where(active, bounce, flat_new[target]))
    fluid = (1 - solid_mask).astype(jnp.float32)
    populations_next = flat_new.reshape(27, Z, NX, NY) * fluid[None]
    momentum = jnp.where(active, toward + bounce, 0.0)
    velocity = jnp.stack([link_dir // 9 - 1, (link_dir // 3) % 3 - 1, link_dir % 3 - 1]).astype(jnp.float32)
    panel_index = jnp.where(active, link_panel, PANELS)
    panel_force = jnp.zeros((3, PANELS), jnp.float32).at[:, panel_index].add(velocity * momentum[None], mode="drop")
    return populations_next, panel_force
```

```python
import functools

import jax
import jax.numpy as jnp
from jax import lax
from jax.experimental import pallas as pl
from jax.experimental.pallas import tpu as pltpu
from jax.sharding import PartitionSpec as P

PAN_DEV = 128
RELAXATION = 1.7
DEPTH, ROWS, COLS = 24, 8, 128
PLANES = DEPTH * ROWS
LINKS = 4096
HALF = DEPTH // 2
CHUNKS = 8
F32 = jnp.float32
BF16 = jnp.bfloat16
VMEM = pltpu.VMEM
WHOLE = pl.BlockSpec(memory_space=pltpu.VMEM)
SOMEWHERE = pl.BlockSpec(memory_space=pl.ANY)


def params(mib):
    return pltpu.CompilerParams(vmem_limit_bytes=mib * 2**20)


def plane_rows(index, z):
    return pl.ds(pl.multiple_of((index * DEPTH + z) * ROWS, ROWS), ROWS)


def inverse_map(m0, m1, m2, u):
    if m0 is None and m1 is None and m2 is None:
        return None, None, None
    w = None if m0 is None else u * m0
    if m1 is not None:
        w = m1 if w is None else w + m1
    t = None
    if w is not None:
        t = u * (w if m1 is None else w + m1)
    if m2 is not None:
        t = m2 if t is None else t + m2
    if w is None:
        return t, -t, t
    return t - w, (-t if m0 is None else m0 - t), t + w


def collide(f):
    def at(a, b, c):
        return f[a * 9 + b * 3 + c]

    ends = [[at(a, b, 2) + at(a, b, 0) for b in range(3)] for a in range(3)]
    dz = [[at(a, b, 2) - at(a, b, 0) for b in range(3)] for a in range(3)]
    s = [[ends[a][b] + at(a, b, 1) for b in range(3)] for a in range(3)]
    row = [s[a][0] + s[a][1] + s[a][2] for a in range(3)]
    density = row[0] + row[1] + row[2]
    q0 = s[0][0] + s[1][0] + s[2][0]
    q2 = s[0][2] + s[1][2] + s[2][2]
    dzx = [dz[a][0] + dz[a][1] + dz[a][2] for a in range(3)]
    dzy0 = dz[0][0] + dz[1][0] + dz[2][0]
    dzy2 = dz[0][2] + dz[1][2] + dz[2][2]
    pzz = sum(ends[a][b] for a in range(3) for b in range(3))
    inv = 1.0 / density
    ux = (row[2] - row[0]) * inv
    uy = (q2 - q0) * inv
    uz = (dzx[0] + dzx[1] + dzx[2]) * inv
    keep = 1.0 - RELAXATION
    third = RELAXATION / 3.0

    def spread(p, first, second):
        return keep * (p * inv - first * second)

    xx = spread(row[2] + row[0], ux, ux) + third
    yy = spread(q2 + q0, uy, uy) + third
    zz = spread(pzz, uz, uz) + third
    xy = spread((s[2][2] - s[2][0]) + (s[0][0] - s[0][2]), ux, uy)
    xz = spread(dzx[2] - dzx[0], ux, uz)
    yz = spread(dzy2 - dzy0, uy, uz)
    xy2, xz2, yz2 = 2.0 * xy, 2.0 * xz, 2.0 * yz
    e220 = xx * yy + xy2 * xy
    e202 = xx * zz + xz2 * xz
    eyz = yy * zz + yz2 * yz
    e211 = xx * yz + xy2 * xz
    e121 = yy * xz + xy2 * yz
    e112 = zz * xy + xz2 * yz
    e222 = xx * eyz + xz2 * e121 + xy2 * e112
    k = {
        (0, 0, 0): jnp.ones_like(density),
        (2, 0, 0): xx,
        (0, 2, 0): yy,
        (0, 0, 2): zz,
        (1, 1, 0): xy,
        (1, 0, 1): xz,
        (0, 1, 1): yz,
        (2, 2, 0): e220,
        (2, 0, 2): e202,
        (0, 2, 2): eyz,
        (2, 1, 1): e211,
        (1, 2, 1): e121,
        (1, 1, 2): e112,
        (2, 2, 2): e222,
    }
    along_z, along_y, result = {}, {}, [None] * 27
    for a in range(3):
        for b in range(3):
            out = inverse_map(k.get((a, b, 0)), k.get((a, b, 1)), k.get((a, b, 2)), uz)
            for c in range(3):
                along_z[a, b, c] = out[c]
    for a in range(3):
        for c in range(3):
            out = inverse_map(along_z[a, 0, c], along_z[a, 1, c], along_z[a, 2, c], uy)
            for b in range(3):
                along_y[a, b, c] = out[b]
    scale = [density, 0.5 * density, 0.25 * density, 0.125 * density]
    for b in range(3):
        for c in range(3):
            out = inverse_map(along_y[0, b, c], along_y[1, b, c], along_y[2, b, c], ux)
            for a in range(3):
                moving = abs(a - 1) + abs(b - 1) + abs(c - 1)
                result[a * 9 + b * 3 + c] = scale[moving] * out[a]
    return result


def collide_kernel(pop_ref, col_ref, near_ref, far_ref, buf, sem):
    even = lax.rem(lax.axis_index("gy"), 2) == 0
    step = DEPTH // CHUNKS
    copies = [
        pltpu.make_async_copy(
            pop_ref.at[:, pl.ds(i * step, step)], buf.at[:, pl.ds(i * step, step)], sem.at[i]
        )
        for i in range(CHUNKS)
    ]
    for copy in copies:
        copy.start()
    lane = lax.broadcasted_iota(jnp.int32, (ROWS, COLS), 1)

    def body(z, carry):
        low, high = carry
        f = collide([buf[d, z] for d in range(27)])
        first = lax.rem(z, HALF) * 9
        for d in range(27):
            col_ref[plane_rows(d, z), :] = f[d]
        for a in range(3):
            for c in range(3):
                spot = first + a * 3 + c
                here = lane == spot
                low = jnp.where(here, pltpu.roll(f[a * 9 + c], spot, 1), low)
                high = jnp.where(here, pltpu.roll(f[a * 9 + 6 + c], spot + 1, 1), high)
        return low, high

    zero = jnp.zeros((ROWS, COLS), F32)
    for half in range(2):
        carry = (zero, zero)
        for i in range(half * CHUNKS // 2, (half + 1) * CHUNKS // 2):
            copies[i].wait()
            carry = lax.fori_loop(i * step, (i + 1) * step, body, carry)
        low, high = carry
        near_ref[half] = jnp.where(even, high, low)
        far_ref[half] = jnp.where(even, low, high)


def side_kernel(col_ref, near_ref, far_ref, side_ref, pair_ref, other_ref, edges):
    even = lax.rem(lax.axis_index("gy"), 2) == 0
    even_x = lax.rem(lax.axis_index("gx"), 2) == 0
    lane = lax.broadcasted_iota(jnp.int32, (ROWS, COLS), 1)
    for half in range(2):
        edges[0, half] = jnp.where(even, far_ref[half], near_ref[half])
        edges[1, half] = jnp.where(even, near_ref[half], far_ref[half])

    def body(z, half):
        first = (z - half * HALF) * 9
        low, high = edges[0, half], edges[1, half]
        for a in range(3):
            for c in range(3):
                spot = first + a * 3 + c
                up = pltpu.roll(col_ref[plane_rows(a * 9 + 6 + c, z), :], 1, 1)
                up = jnp.where(lane == 0, pltpu.roll(low, COLS - spot, 1), up)
                side_ref[plane_rows(a * 6 + 3 + c, z), :] = up
                down = pltpu.roll(col_ref[plane_rows(a * 9 + c, z), :], COLS - 1, 1)
                down = jnp.where(
                    lane == COLS - 1, pltpu.roll(high, COLS - 1 - spot, 1), down
                )
                side_ref[plane_rows(a * 6 + c, z), :] = down
        return half

    for half in range(2):
        lax.fori_loop(half * HALF, (half + 1) * HALF, body, half)
    for ref, forward in ((pair_ref, even_x), (other_ref, jnp.logical_not(even_x))):
        a = jnp.where(forward, 2, 0)
        x = jnp.where(forward, ROWS - 1, 0)
        for b in range(3):
            for c in range(3):
                if b == 1:
                    source, start = col_ref, (a * 9 + 3 + c) * PLANES + x
                else:
                    source, start = side_ref, (a * 6 + (b // 2) * 3 + c) * PLANES + x
                ref[b * 3 + c] = source[pl.ds(start, DEPTH, stride=ROWS), :]


def table_kernel(cell_ref, dir_ref, q_ref, panel_ref, dense_ref, row_ref, lane_ref, pan_ref, push_ref):
    gx = lax.axis_index("gx")
    count = lax.axis_size("gx")
    per_row = PAN_DEV * lax.axis_size("gy")
    width = 256
    row_iota = lax.broadcasted_iota(jnp.int32, (PLANES, width), 0)
    lane_iota = lax.broadcasted_iota(jnp.int32, (COLS, width), 0)
    push_iota = lax.broadcasted_iota(jnp.int32, (24, width), 0)
    dense_ref[...] = jnp.zeros_like(dense_ref)

    def load(ref, i):
        return jnp.concatenate([ref[pl.ds(2 * i, 1), :], ref[pl.ds(2 * i + 1, 1), :]], axis=1)

    def body(i, carry):
        at = pl.ds(pl.multiple_of(i * width, width), width)
        cell, direction = load(cell_ref, i), load(dir_ref, i)
        q, panel = load(q_ref, i), load(panel_ref, i)
        active = panel >= 0
        near = q < 0.5
        twice = 2.0 * q
        weight = jnp.where(near, twice, 1.0 / twice)
        weight_hi = weight.astype(BF16).astype(F32)
        weight_lo = weight - weight_hi
        code = (direction + 1 + jnp.where(near, 27, 0)).astype(F32)
        row = jnp.where(active, cell // COLS, -1)
        rows = jnp.where(row_iota == row, 1.0, 0.0).astype(BF16)
        row_ref[:, at] = rows
        here = lane_iota == cell % COLS
        lane_ref[:, at] = jnp.where(here, 1.0, 0.0).astype(BF16)
        values = jnp.concatenate(
            [jnp.where(here, v, 0.0).astype(BF16) for v in (weight_hi, weight_lo, code)], axis=0
        )
        dense_ref[...] += lax.dot_general(
            rows, values, (((1,), (1,)), ((), ())), preferred_element_type=F32
        )
        pan_ref[:, at] = jnp.where(lane_iota == panel % PAN_DEV, 1.0, 0.0).astype(BF16)
        offset = panel // per_row - gx + 1
        offset = jnp.where(offset < 0, offset + count, offset)
        offset = jnp.where(offset >= count, offset - count, offset)
        part = push_iota % 8
        step = jnp.where(
            part == 0,
            direction // 9 - 1,
            jnp.where(part == 1, direction // 3 % 3 - 1, direction % 3 - 1),
        )
        chosen = active & (push_iota // 8 == offset) & (part < 3)
        push_ref[:, at] = jnp.where(chosen, step, 0).astype(F32)
        return carry

    lax.fori_loop(0, LINKS // width, body, 0)


def stream_kernel(
    col_ref, side_ref, pair_ref, other_ref, dense_ref, row_ref, lane_ref, pan_ref, push_ref, mask_ref,
    out_ref, own_ref, send_pair_ref, send_other_ref,
    buf, halo, momentum, sem,
):
    even_x = lax.rem(lax.axis_index("gx"), 2) == 0
    halo[0] = jnp.where(even_x, other_ref[...], pair_ref[...])
    halo[1] = jnp.where(even_x, pair_ref[...], other_ref[...])
    sub = lax.broadcasted_iota(jnp.int32, (ROWS, COLS), 0)

    def body(z, bottom, top):
        code = dense_ref[pl.ds(pl.multiple_of(z * ROWS, ROWS), ROWS), 2 * COLS : 3 * COLS]
        weight = (
            dense_ref[pl.ds(pl.multiple_of(z * ROWS, ROWS), ROWS), :COLS]
            + dense_ref[pl.ds(pl.multiple_of(z * ROWS, ROWS), ROWS), COLS : 2 * COLS]
        )
        fluid = (1 - mask_ref[z]).astype(F32)
        near = code > 27.5
        which = jnp.where(near, code - 28.0, code - 1.0)
        toward = jnp.zeros((ROWS, COLS), F32)
        second, reverse = toward, toward
        for d in range(27):
            a, b, c = d // 9, d // 3 % 3, d % 3
            here = col_ref[plane_rows(d, z), :]
            back = col_ref[plane_rows(26 - d, z), :]
            if (c == 2 and bottom) or (c == 0 and top):
                moved = back
            else:
                zs = z - (c - 1)
                if b == 1:
                    moved = col_ref[plane_rows(d, zs), :]
                else:
                    moved = side_ref[plane_rows(a * 6 + (b // 2) * 3 + c, zs), :]
                if a == 2:
                    edge = halo[0, b * 3 + c, pl.ds(zs, 1), :]
                    moved = jnp.where(sub == 0, edge, pltpu.roll(moved, 1, 0))
                elif a == 0:
                    edge = halo[1, b * 3 + c, pl.ds(zs, 1), :]
                    moved = jnp.where(sub == ROWS - 1, edge, pltpu.roll(moved, ROWS - 1, 0))
            buf[d, z] = moved
            if d != 13:
                match = which == float(d)
                toward = jnp.where(match, here, toward)
                second = jnp.where(match, moved, second)
                reverse = jnp.where(match, back, reverse)
        other = jnp.where(near, second, reverse)
        bounce = other + weight * (toward - other)
        momentum[pl.ds(pl.multiple_of(z * ROWS, ROWS), ROWS), :] = jnp.where(
            code > 0.5, toward + bounce, 0.0
        )
        for d in range(27):
            value = buf[d, z]
            if d != 13:
                value = jnp.where(which == float(26 - d), bounce, value)
            buf[d, z] = value * fluid

    body(0, True, False)
    lax.fori_loop(1, DEPTH - 1, lambda z, carry: (body(z, False, False), carry)[1], 0)
    body(DEPTH - 1, False, True)
    copy = pltpu.make_async_copy(buf, out_ref, sem)
    copy.start()

    turned = momentum[...].T
    turned_hi = turned.astype(BF16)
    turned_lo = (turned - turned_hi.astype(F32)).astype(BF16)
    width = 512

    def gather(i, total):
        at = pl.ds(pl.multiple_of(i * width, width), width)
        rows = row_ref[:, at]
        picked = jnp.dot(turned_hi, rows, preferred_element_type=F32) + jnp.dot(
            turned_lo, rows, preferred_element_type=F32
        )
        value = jnp.sum(picked * lane_ref[:, at].astype(F32), axis=0, keepdims=True)
        push = push_ref[:, at] * value
        push_hi = push.astype(BF16).astype(F32)
        push = jnp.concatenate([push_hi, push - push_hi], axis=0).astype(BF16)
        return total + lax.dot_general(
            push, pan_ref[:, at], (((1,), (1,)), ((), ())), preferred_element_type=F32
        )

    total = lax.fori_loop(0, LINKS // width, gather, jnp.zeros((48, PAN_DEV), F32))
    force = total[:24] + total[24:]
    own_ref[...] = force[8:16]
    send_pair_ref[...] = jnp.where(even_x, force[16:24], force[0:8])
    send_other_ref[...] = jnp.where(even_x, force[0:8], force[16:24])
    copy.wait()


def pair_swap(count):
    return [(i, i ^ 1) for i in range(count)]


def other_swap(count):
    return [(i, (i + 1) % count if i % 2 else (i - 1) % count) for i in range(count)]


def per_device(populations, solid_mask, link_cell, link_dir, link_second, link_q, link_panel):
    nx, ny = lax.axis_size("gx"), lax.axis_size("gy")
    small = jax.ShapeDtypeStruct((ROWS, PAN_DEV), F32)
    column = jax.ShapeDtypeStruct((2, ROWS, COLS), F32)
    edge = jax.ShapeDtypeStruct((9, DEPTH, COLS), F32)
    collided, y_pair, y_other = pl.pallas_call(
        collide_kernel,
        out_shape=(VMEM((27 * PLANES, COLS), F32), column, column),
        in_specs=[SOMEWHERE],
        scratch_shapes=[VMEM((27, DEPTH, ROWS, COLS), F32), pltpu.SemaphoreType.DMA((CHUNKS,))],
        compiler_params=params(16),
        name="collide",
    )(populations)
    y_other = lax.ppermute(y_other, "gy", other_swap(ny))
    y_pair = lax.ppermute(y_pair, "gy", pair_swap(ny))
    tables = [t.reshape(LINKS // COLS, COLS) for t in (link_cell, link_dir, link_q, link_panel)]
    dense = pl.pallas_call(
        table_kernel,
        out_shape=(
            VMEM((PLANES, 3 * COLS), F32),
            VMEM((PLANES, LINKS), BF16),
            VMEM((COLS, LINKS), BF16),
            VMEM((PAN_DEV, LINKS), BF16),
            VMEM((24, LINKS), F32),
        ),
        in_specs=[WHOLE] * 4,
        compiler_params=params(16),
        cost_estimate=pl.CostEstimate(flops=6 * 10**9, bytes_accessed=70000, transcendentals=0),
        name="tables",
    )(*tables)
    side, x_pair, x_other = pl.pallas_call(
        side_kernel,
        out_shape=(VMEM((18 * PLANES, COLS), F32), edge, edge),
        in_specs=[WHOLE] * 3,
        scratch_shapes=[VMEM((2, 2, ROWS, COLS), F32)],
        compiler_params=params(16),
        name="sides",
    )(collided, y_pair, y_other)
    x_other = lax.ppermute(x_other, "gx", other_swap(nx))
    x_pair = lax.ppermute(x_pair, "gx", pair_swap(nx))
    populations_next, own, to_pair, to_other = pl.pallas_call(
        stream_kernel,
        out_shape=(jax.ShapeDtypeStruct(populations.shape, F32), small, small, small),
        in_specs=[WHOLE] * 10,
        out_specs=(SOMEWHERE, WHOLE, WHOLE, WHOLE),
        scratch_shapes=[
            VMEM((27, DEPTH, ROWS, COLS), F32),
            VMEM((2, 9, DEPTH, COLS), F32),
            VMEM((PLANES, COLS), F32),
            pltpu.SemaphoreType.DMA,
        ],
        compiler_params=params(24),
        name="stream",
    )(collided, side, x_pair, x_other, *dense, solid_mask)
    from_other = lax.ppermute(to_other, "gx", other_swap(nx))
    from_pair = lax.ppermute(to_pair, "gx", pair_swap(nx))
    return populations_next, (own + from_pair + from_other)[:3]


def solution(mesh):
    return jax.shard_map(
        per_device,
        mesh=mesh,
        in_specs=(
            P(None, None, "gx", "gy"),
            P(None, "gx", "gy"),
            P(("gx", "gy")),
            P(("gx", "gy")),
            P(("gx", "gy")),
            P(("gx", "gy")),
            P(("gx", "gy")),
        ),
        out_specs=(P(None, None, "gx", "gy"), P(None, ("gx", "gy"))),
        check_vma=False,
    )
```

```python
import functools

import jax
import jax.numpy as jnp
from jax import lax
from jax.experimental import pallas as pl
from jax.experimental.pallas import tpu as pltpu
from jax.sharding import PartitionSpec as P

PAN_DEV = 128
RELAXATION = 1.7
DEPTH, ROWS, COLS = 24, 8, 128
PLANES = DEPTH * ROWS
LINKS = 4096
HALF = DEPTH // 2
CHUNKS = 4
UNROLL_A = 6
UNROLL_T = 8
UNROLL_S = 11
UNROLL_G = 4
TABLE_WIDTH = 512
GATHER_WIDTH = 1024
F32 = jnp.float32
BF16 = jnp.bfloat16
VMEM = pltpu.VMEM
WHOLE = pl.BlockSpec(memory_space=pltpu.VMEM)
SOMEWHERE = pl.BlockSpec(memory_space=pl.ANY)
HBM = pl.BlockSpec(memory_space=pltpu.HBM)


def params(mib):
    return pltpu.CompilerParams(vmem_limit_bytes=mib * 2**20)


def plane_rows(index, z):
    return pl.ds(pl.multiple_of((index * DEPTH + z) * ROWS, ROWS), ROWS)


def inverse_map(m0, m1, m2, u):
    if m0 is None and m1 is None and m2 is None:
        return None, None, None
    w = None if m0 is None else u * m0
    if m1 is not None:
        w = m1 if w is None else w + m1
    t = None
    if w is not None:
        t = u * (w if m1 is None else w + m1)
    if m2 is not None:
        t = m2 if t is None else t + m2
    if w is None:
        return t, -t, t
    return t - w, (-t if m0 is None else m0 - t), t + w


def collide(f):
    def at(a, b, c):
        return f[a * 9 + b * 3 + c]

    ends = [[at(a, b, 2) + at(a, b, 0) for b in range(3)] for a in range(3)]
    dz = [[at(a, b, 2) - at(a, b, 0) for b in range(3)] for a in range(3)]
    s = [[ends[a][b] + at(a, b, 1) for b in range(3)] for a in range(3)]
    row = [s[a][0] + s[a][1] + s[a][2] for a in range(3)]
    density = row[0] + row[1] + row[2]
    q0 = s[0][0] + s[1][0] + s[2][0]
    q2 = s[0][2] + s[1][2] + s[2][2]
    dzx = [dz[a][0] + dz[a][1] + dz[a][2] for a in range(3)]
    dzy0 = dz[0][0] + dz[1][0] + dz[2][0]
    dzy2 = dz[0][2] + dz[1][2] + dz[2][2]
    pzz = sum(ends[a][b] for a in range(3) for b in range(3))
    inv = 1.0 / density
    ux = (row[2] - row[0]) * inv
    uy = (q2 - q0) * inv
    uz = (dzx[0] + dzx[1] + dzx[2]) * inv
    keep = 1.0 - RELAXATION
    third = RELAXATION / 3.0

    def spread(p, first, second):
        return keep * (p * inv - first * second)

    xx = spread(row[2] + row[0], ux, ux) + third
    yy = spread(q2 + q0, uy, uy) + third
    zz = spread(pzz, uz, uz) + third
    xy = spread((s[2][2] - s[2][0]) + (s[0][0] - s[0][2]), ux, uy)
    xz = spread(dzx[2] - dzx[0], ux, uz)
    yz = spread(dzy2 - dzy0, uy, uz)
    xy2, xz2, yz2 = 2.0 * xy, 2.0 * xz, 2.0 * yz
    e220 = xx * yy + xy2 * xy
    e202 = xx * zz + xz2 * xz
    eyz = yy * zz + yz2 * yz
    e211 = xx * yz + xy2 * xz
    e121 = yy * xz + xy2 * yz
    e112 = zz * xy + xz2 * yz
    e222 = xx * eyz + xz2 * e121 + xy2 * e112
    k = {
        (0, 0, 0): jnp.ones_like(density),
        (2, 0, 0): xx,
        (0, 2, 0): yy,
        (0, 0, 2): zz,
        (1, 1, 0): xy,
        (1, 0, 1): xz,
        (0, 1, 1): yz,
        (2, 2, 0): e220,
        (2, 0, 2): e202,
        (0, 2, 2): eyz,
        (2, 1, 1): e211,
        (1, 2, 1): e121,
        (1, 1, 2): e112,
        (2, 2, 2): e222,
    }
    along_z, along_y, result = {}, {}, [None] * 27
    for a in range(3):
        for b in range(3):
            out = inverse_map(k.get((a, b, 0)), k.get((a, b, 1)), k.get((a, b, 2)), uz)
            for c in range(3):
                along_z[a, b, c] = out[c]
    for a in range(3):
        for c in range(3):
            out = inverse_map(along_z[a, 0, c], along_z[a, 1, c], along_z[a, 2, c], uy)
            for b in range(3):
                along_y[a, b, c] = out[b]
    scale = [density, 0.5 * density, 0.25 * density, 0.125 * density]
    for b in range(3):
        for c in range(3):
            out = inverse_map(along_y[0, b, c], along_y[1, b, c], along_y[2, b, c], ux)
            for a in range(3):
                moving = abs(a - 1) + abs(b - 1) + abs(c - 1)
                result[a * 9 + b * 3 + c] = scale[moving] * out[a]
    return result


def collide_kernel(pop_ref, col_ref, near_ref, far_ref, buf, sem):
    even = lax.rem(lax.axis_index("gy"), 2) == 0
    step = DEPTH // CHUNKS
    copies = [
        pltpu.make_async_copy(
            pop_ref.at[:, pl.ds(i * step, step)], buf.at[:, pl.ds(i * step, step)], sem.at[i]
        )
        for i in range(CHUNKS)
    ]
    for copy in copies:
        copy.start()
    lane = lax.broadcasted_iota(jnp.int32, (ROWS, COLS), 1)

    def body(z, carry):
        low, high = carry
        f = collide([buf[d, z] for d in range(27)])
        first = lax.rem(z, HALF) * 9
        for d in range(27):
            col_ref[plane_rows(d, z), :] = f[d]
        for a in range(3):
            for c in range(3):
                spot = first + a * 3 + c
                here = lane == spot
                low = jnp.where(here, pltpu.roll(f[a * 9 + c], spot, 1), low)
                high = jnp.where(here, pltpu.roll(f[a * 9 + 6 + c], spot + 1, 1), high)
        return low, high

    zero = jnp.zeros((ROWS, COLS), F32)
    for half in range(2):
        carry = (zero, zero)
        for i in range(half * CHUNKS // 2, (half + 1) * CHUNKS // 2):
            copies[i].wait()
            carry = lax.fori_loop(i * step, (i + 1) * step, body, carry, unroll=UNROLL_A)
        low, high = carry
        near_ref[pl.ds(half * ROWS, ROWS), :] = jnp.where(even, high, low)
        far_ref[pl.ds(half * ROWS, ROWS), :] = jnp.where(even, low, high)
    wide = lax.broadcasted_iota(jnp.int32, (DEPTH, COLS), 1)
    low = jnp.zeros((DEPTH, COLS), F32)
    high = low
    for end in range(2):
        for c in range(3):
            spot = end * 3 + c
            start = (end * 18 + c) * PLANES + end * (ROWS - 1)
            column = col_ref[pl.ds(start, DEPTH, stride=ROWS), :]
            low = jnp.where(wide == spot, pltpu.roll(column, spot, 1), low)
            column = col_ref[pl.ds(start + 6 * PLANES, DEPTH, stride=ROWS), :]
            high = jnp.where(wide == spot, pltpu.roll(column, spot + 1, 1), high)
    near_ref[2 * ROWS :, :] = jnp.where(even, high, low)
    far_ref[2 * ROWS :, :] = jnp.where(even, low, high)


def edge_kernel(col_ref, near_ref, far_ref, pair_ref, other_ref):
    even = lax.rem(lax.axis_index("gy"), 2) == 0
    even_x = lax.rem(lax.axis_index("gx"), 2) == 0
    lane = lax.broadcasted_iota(jnp.int32, (DEPTH, COLS), 1)
    low = jnp.where(even, far_ref[2 * ROWS :, :], near_ref[2 * ROWS :, :])
    high = jnp.where(even, near_ref[2 * ROWS :, :], far_ref[2 * ROWS :, :])
    for end in range(2):
        rows = []
        for b in range(3):
            for c in range(3):
                start = (end * 18 + b * 3 + c) * PLANES + end * (ROWS - 1)
                row = col_ref[pl.ds(start, DEPTH, stride=ROWS), :]
                spot = end * 3 + c
                if b == 2:
                    halo = pltpu.roll(low, (COLS - spot) % COLS, 1)
                    row = jnp.where(lane == 0, halo, pltpu.roll(row, 1, 1))
                elif b == 0:
                    halo = pltpu.roll(high, COLS - 1 - spot, 1)
                    row = jnp.where(lane == COLS - 1, halo, pltpu.roll(row, COLS - 1, 1))
                rows.append(row)

        @pl.when(even_x == (end == 1))
        def _():
            for k in range(9):
                pair_ref[k] = rows[k]

        @pl.when(even_x != (end == 1))
        def _():
            for k in range(9):
                other_ref[k] = rows[k]


def table_kernel(
    cell_ref, dir_ref, q_ref, panel_ref, dense_ref, row_ref, lane_ref, pan_ref, push_ref, gathered
):
    gx = lax.axis_index("gx")
    count = lax.axis_size("gx")
    per_row = PAN_DEV * lax.axis_size("gy")
    width = TABLE_WIDTH
    row_iota = lax.broadcasted_iota(jnp.int32, (PLANES, width), 0)
    lane_iota = lax.broadcasted_iota(jnp.int32, (COLS, width), 0)
    push_iota = lax.broadcasted_iota(jnp.int32, (24, width), 0)
    gathered[...] = jnp.zeros_like(gathered)

    def load(ref, i):
        n = width // COLS
        return jnp.concatenate([ref[pl.ds(n * i + j, 1), :] for j in range(n)], axis=1)

    def body(i, carry):
        at = pl.ds(pl.multiple_of(i * width, width), width)
        cell, direction = load(cell_ref, i), load(dir_ref, i)
        q, panel = load(q_ref, i), load(panel_ref, i)
        active = panel >= 0
        near = q < 0.5
        twice = 2.0 * q
        weight = jnp.where(near, twice, 1.0 / twice)
        weight_hi = weight.astype(BF16).astype(F32)
        weight_lo = weight - weight_hi
        offset = panel // per_row - gx + 1
        offset = jnp.where(offset < 0, offset + count, offset)
        offset = jnp.where(offset >= count, offset - count, offset)
        code = (direction + 1 + jnp.where(near, 27, 0) + 54 * offset).astype(F32)
        spot = panel % PAN_DEV
        row = jnp.where(active, cell // COLS, -1)
        rows = jnp.where(row_iota == row, 1.0, 0.0).astype(BF16)
        row_ref[:, at] = rows
        here = lane_iota == cell % COLS
        lane_ref[:, at] = jnp.where(here, 1.0, 0.0).astype(BF16)
        values = jnp.concatenate(
            [
                jnp.where(here, v, 0.0).astype(BF16)
                for v in (weight_hi, weight_lo, code, spot.astype(F32))
            ],
            axis=0,
        )
        gathered[...] += lax.dot_general(
            rows, values, (((1,), (1,)), ((), ())), preferred_element_type=F32
        )
        pan_ref[:, at] = jnp.where(lane_iota == spot, 1.0, 0.0).astype(BF16)
        part = push_iota % 8
        step = jnp.where(
            part == 0,
            direction // 9 - 1,
            jnp.where(part == 1, direction // 3 % 3 - 1, direction % 3 - 1),
        )
        chosen = active & (push_iota // 8 == offset) & (part < 3)
        push_ref[:, at] = jnp.where(chosen, step, 0).astype(F32)
        return carry

    lax.fori_loop(0, LINKS // width, body, 0, unroll=UNROLL_T)
    dense_ref[:PLANES, :] = gathered[:, :COLS] + gathered[:, COLS : 2 * COLS]
    dense_ref[PLANES : 2 * PLANES, :] = gathered[:, 2 * COLS : 3 * COLS]
    dense_ref[2 * PLANES :, :] = gathered[:, 3 * COLS :]


def split_code(code):
    offset = jnp.where(code > 108.5, 2.0, jnp.where(code > 54.5, 1.0, 0.0))
    code = code - 54.0 * offset
    near = code > 27.5
    return offset, near, jnp.where(near, code - 28.0, code - 1.0)


def by_panel(push, pan):
    push_hi = push.astype(BF16).astype(F32)
    push = jnp.concatenate([push_hi, push - push_hi], axis=0).astype(BF16)
    return lax.dot_general(push, pan, (((1,), (1,)), ((), ())), preferred_element_type=F32)


def stream_kernel(
    col_ref, near_ref, far_ref, pair_ref, dense_ref, row_ref, lane_ref, pan_ref, push_ref, mask_ref,
    new_ref, force_ref, late_push_ref, late_pan_ref,
    edges, halo, momentum,
):
    even = lax.rem(lax.axis_index("gy"), 2) == 0
    even_x = lax.rem(lax.axis_index("gx"), 2) == 0
    halo[0] = jnp.where(even_x, 0.0, pair_ref[...])
    halo[1] = jnp.where(even_x, pair_ref[...], 0.0)
    for half in range(2):
        at = pl.ds(half * ROWS, ROWS)
        edges[0, half] = jnp.where(even, far_ref[at, :], near_ref[at, :])
        edges[1, half] = jnp.where(even, near_ref[at, :], far_ref[at, :])
    sub = lax.broadcasted_iota(jnp.int32, (ROWS, COLS), 0)
    lane = lax.broadcasted_iota(jnp.int32, (ROWS, COLS), 1)

    def body(z, bottom, top):
        here_rows = pl.ds(pl.multiple_of(z * ROWS, ROWS), ROWS)
        code = dense_ref[pl.ds(pl.multiple_of(PLANES + z * ROWS, ROWS), ROWS), :]
        weight = dense_ref[here_rows, :]
        fluid = (1 - mask_ref[z]).astype(F32)
        offset, near, which = split_code(code)
        toward = jnp.zeros((ROWS, COLS), F32)
        second, reverse = toward, toward
        for d in range(27):
            a, b, c = d // 9, d // 3 % 3, d % 3
            here = col_ref[plane_rows(d, z), :]
            back = col_ref[plane_rows(26 - d, z), :]
            if (c == 2 and bottom) or (c == 0 and top):
                moved = back
            else:
                zs = z - (c - 1)
                moved = col_ref[plane_rows(d, zs), :]
                half = jnp.where(zs < HALF, 0, 1)
                spot = (zs - half * HALF) * 9 + a * 3 + c
                if b == 2:
                    side = pltpu.roll(edges[0, half], COLS - spot, 1)
                    moved = jnp.where(lane == 0, side, pltpu.roll(moved, 1, 1))
                elif b == 0:
                    side = pltpu.roll(edges[1, half], COLS - 1 - spot, 1)
                    moved = jnp.where(lane == COLS - 1, side, pltpu.roll(moved, COLS - 1, 1))
                if a == 2:
                    edge = halo[0, b * 3 + c, pl.ds(zs, 1), :]
                    moved = jnp.where(sub == 0, edge, pltpu.roll(moved, 1, 0))
                elif a == 0:
                    edge = halo[1, b * 3 + c, pl.ds(zs, 1), :]
                    moved = jnp.where(sub == ROWS - 1, edge, pltpu.roll(moved, ROWS - 1, 0))
            new_ref[plane_rows(d, z), :] = moved
            if d != 13:
                match = which == float(d)
                toward = jnp.where(match, here, toward)
                second = jnp.where(match, moved, second)
                reverse = jnp.where(match, back, reverse)
        other = jnp.where(near, second, reverse)
        bounce = other + weight * (toward - other)
        momentum[here_rows, :] = jnp.where(code > 0.5, toward + bounce, 0.0)
        for d in range(27):
            value = new_ref[plane_rows(d, z), :]
            if d != 13:
                value = jnp.where(which == float(26 - d), bounce, value)
            new_ref[plane_rows(d, z), :] = value * fluid

    body(0, True, False)
    lax.fori_loop(
        1, DEPTH - 1, lambda z, carry: (body(z, False, False), carry)[1], 0, unroll=UNROLL_S
    )
    body(DEPTH - 1, False, True)

    turned = momentum[...].T
    turned_hi = turned.astype(BF16)
    turned_lo = (turned - turned_hi.astype(F32)).astype(BF16)
    width = GATHER_WIDTH

    def gather(i, total):
        at = pl.ds(pl.multiple_of(i * width, width), width)
        rows = row_ref[:, at]
        picked = jnp.dot(turned_hi, rows, preferred_element_type=F32) + jnp.dot(
            turned_lo, rows, preferred_element_type=F32
        )
        value = jnp.sum(picked * lane_ref[:, at].astype(F32), axis=0, keepdims=True)
        return total + by_panel(push_ref[:, at] * value, pan_ref[:, at])

    total = lax.fori_loop(
        0, LINKS // width, gather, jnp.zeros((48, PAN_DEV), F32), unroll=UNROLL_G
    )
    force_ref[...] = total[:24] + total[24:]

    last = jnp.where(even_x, 0, ROWS - 1)
    picked = [dense_ref[pl.ds(i * PLANES + last, DEPTH, stride=ROWS), :] for i in range(3)]
    offset, near, which = split_code(picked[1])
    lead = jnp.where(even_x, 18.0, 0.0)
    across = near & (which >= lead) & (which < lead + 9.0)
    share = jnp.where(across, 1.0 - picked[0], 0.0)
    k = jnp.where(across, which - lead, 0.0)
    step_y = jnp.where(k > 5.5, 1.0, jnp.where(k > 2.5, 0.0, -1.0))
    step_z = k - 3.0 * step_y - 4.0
    step_x = jnp.where(even_x, share, -share)
    step_y, step_z = step_y * share, step_z * share
    push_iota = lax.broadcasted_iota(jnp.int32, (24, COLS), 0)
    part, owner = push_iota % 8, (push_iota // 8).astype(F32)
    pan_iota = lax.broadcasted_iota(jnp.int32, (PAN_DEV, COLS), 0).astype(F32)
    for z in range(DEPTH):
        row = slice(z, z + 1)
        steps = jnp.where(
            part == 0,
            step_x[row],
            jnp.where(part == 1, step_y[row], jnp.where(part == 2, step_z[row], 0.0)),
        )
        at = slice(z * COLS, (z + 1) * COLS)
        late_push_ref[:, at] = jnp.where(owner == offset[row], steps, 0.0)
        late_pan_ref[:, at] = jnp.where(pan_iota == picked[2][row], 1.0, 0.0).astype(BF16)


def late_row(dense_ref, even_x):
    last = jnp.where(even_x, 0, ROWS - 1)
    weight = dense_ref[pl.ds(last, DEPTH, stride=ROWS), :]
    _, near, which = split_code(dense_ref[pl.ds(PLANES + last, DEPTH, stride=ROWS), :])
    return near, which, weight


def late_kernel(other_ref, dense_ref, force_ref, late_push_ref, late_pan_ref, own_ref, send_pair_ref, send_other_ref):
    even_x = lax.rem(lax.axis_index("gx"), 2) == 0
    near, which, weight = late_row(dense_ref, even_x)
    lead = jnp.where(even_x, 18.0, 0.0)
    second = jnp.zeros((DEPTH, COLS), F32)
    for k in range(9):
        row = other_ref[k]
        if k % 3 == 2:
            row = pltpu.roll(row, 1, 0)
        elif k % 3 == 0:
            row = pltpu.roll(row, DEPTH - 1, 0)
        second = jnp.where(which == lead + float(k), row, second)
    second = jnp.concatenate([second[z : z + 1] for z in range(DEPTH)], axis=1)
    late = by_panel(late_push_ref[...] * second, late_pan_ref[...])
    force = force_ref[...] + late[:24] + late[24:]
    own_ref[...] = force[8:16]
    send_pair_ref[...] = jnp.where(even_x, force[16:24], force[0:8])
    send_other_ref[...] = jnp.where(even_x, force[0:8], force[16:24])


def finish_kernel(new_in_ref, other_ref, dense_ref, mask_ref, out_ref, new_ref, sem):
    del new_in_ref
    even_x = lax.rem(lax.axis_index("gx"), 2) == 0
    near, which, weight = late_row(dense_ref, even_x)
    last = jnp.where(even_x, 0, ROWS - 1)
    lead_index = jnp.where(even_x, 18, 0)
    lead = lead_index.astype(F32)
    fluid = (1 - mask_ref[pl.ds(last, DEPTH, stride=ROWS), :]).astype(F32)
    level = lax.broadcasted_iota(jnp.int32, (DEPTH, COLS), 0)
    for k in range(9):
        row = other_ref[k]
        inside = level >= 0
        if k % 3 == 2:
            row = pltpu.roll(row, 1, 0)
            inside = level > 0
        elif k % 3 == 0:
            row = pltpu.roll(row, DEPTH - 1, 0)
            inside = level < DEPTH - 1
        row = row * fluid
        index = lead_index + k
        at = pl.ds(index * PLANES + last, DEPTH, stride=ROWS)
        free = inside & (which != 26.0 - lead - float(k))
        new_ref[at, :] = jnp.where(free, row, new_ref[at, :])
        at = pl.ds((26 - index) * PLANES + last, DEPTH, stride=ROWS)
        hit = near & (which == lead + float(k))
        new_ref[at, :] = new_ref[at, :] + jnp.where(hit, (1.0 - weight) * row, 0.0)
    copy = pltpu.make_async_copy(new_ref, out_ref, sem)
    copy.start()
    copy.wait()


def pair_swap(count):
    return [(i, i ^ 1) for i in range(count)]


def other_swap(count):
    return [(i, (i + 1) % count if i % 2 else (i - 1) % count) for i in range(count)]


def per_device(populations, solid_mask, link_cell, link_dir, link_second, link_q, link_panel):
    nx, ny = lax.axis_size("gx"), lax.axis_size("gy")
    small = jax.ShapeDtypeStruct((ROWS, PAN_DEV), F32)
    column = jax.ShapeDtypeStruct((2 * ROWS + DEPTH, COLS), F32)
    edge = jax.ShapeDtypeStruct((9, DEPTH, COLS), F32)
    collided, y_pair, y_other = pl.pallas_call(
        collide_kernel,
        out_shape=(VMEM((27 * PLANES, COLS), F32), column, column),
        in_specs=[HBM],
        scratch_shapes=[VMEM((27, DEPTH, ROWS, COLS), F32), pltpu.SemaphoreType.DMA((CHUNKS,))],
        compiler_params=params(16),
        name="collide",
    )(pltpu.with_memory_space_constraint(populations, pltpu.HBM))
    y_other = lax.ppermute(y_other, "gy", other_swap(ny))
    y_pair = lax.ppermute(y_pair, "gy", pair_swap(ny))
    x_pair, x_other = pl.pallas_call(
        edge_kernel,
        out_shape=(edge, edge),
        in_specs=[WHOLE] * 3,
        compiler_params=params(16),
        name="edges",
    )(collided, y_pair, y_other)
    x_other = lax.ppermute(x_other, "gx", other_swap(nx))
    x_pair = lax.ppermute(x_pair, "gx", pair_swap(nx))
    tables = [t.reshape(LINKS // COLS, COLS) for t in (link_cell, link_dir, link_q, link_panel)]
    tables = pl.pallas_call(
        table_kernel,
        out_shape=(
            VMEM((3 * PLANES, COLS), F32),
            VMEM((PLANES, LINKS), BF16),
            VMEM((COLS, LINKS), BF16),
            VMEM((PAN_DEV, LINKS), BF16),
            VMEM((24, LINKS), F32),
        ),
        in_specs=[WHOLE] * 4,
        scratch_shapes=[VMEM((PLANES, 4 * COLS), F32)],
        compiler_params=params(16),
        cost_estimate=pl.CostEstimate(flops=6 * 10**9, bytes_accessed=70000, transcendentals=0),
        name="tables",
    )(*tables)
    dense = tables[0]
    moved, force, late_push, late_pan = pl.pallas_call(
        stream_kernel,
        out_shape=(
            VMEM((27 * PLANES, COLS), F32),
            VMEM((24, PAN_DEV), F32),
            VMEM((24, DEPTH * COLS), F32),
            VMEM((PAN_DEV, DEPTH * COLS), BF16),
        ),
        in_specs=[WHOLE] * 10,
        scratch_shapes=[
            VMEM((2, 2, ROWS, COLS), F32),
            VMEM((2, 9, DEPTH, COLS), F32),
            VMEM((PLANES, COLS), F32),
        ],
        compiler_params=params(24),
        name="stream",
    )(collided, y_pair, y_other, x_pair, *tables, solid_mask)
    own, to_pair, to_other = pl.pallas_call(
        late_kernel,
        out_shape=(small, small, small),
        in_specs=[WHOLE] * 5,
        compiler_params=params(16),
        name="late",
    )(x_other, dense, force, late_push, late_pan)
    from_other = lax.ppermute(to_other, "gx", other_swap(nx))
    from_pair = lax.ppermute(to_pair, "gx", pair_swap(nx))
    populations_next, _ = pl.pallas_call(
        finish_kernel,
        out_shape=(
            jax.ShapeDtypeStruct((27 * PLANES, COLS), F32),
            VMEM((27 * PLANES, COLS), F32),
        ),
        in_specs=[WHOLE] * 4,
        out_specs=(SOMEWHERE, WHOLE),
        input_output_aliases={0: 1},
        scratch_shapes=[pltpu.SemaphoreType.DMA],
        compiler_params=params(16),
        name="finish",
    )(moved, x_other, dense, solid_mask.reshape(PLANES, COLS))
    return populations_next.reshape(populations.shape), (own + from_pair + from_other)[:3]


def solution(mesh):
    return jax.shard_map(
        per_device,
        mesh=mesh,
        in_specs=(
            P(None, None, "gx", "gy"),
            P(None, "gx", "gy"),
            P(("gx", "gy")),
            P(("gx", "gy")),
            P(("gx", "gy")),
            P(("gx", "gy")),
            P(("gx", "gy")),
        ),
        out_specs=(P(None, None, "gx", "gy"), P(None, ("gx", "gy"))),
        check_vma=False,
    )
```

```python
import functools

import jax
import jax.numpy as jnp
from jax import lax
from jax.experimental import pallas as pl
from jax.experimental.pallas import tpu as pltpu
from jax.sharding import PartitionSpec as P

PAN_DEV = 128
RELAXATION = 1.7
DEPTH, ROWS, COLS = 24, 8, 128
PLANES = DEPTH * ROWS
LINKS = 4096
HALF = DEPTH // 2
CHUNKS = 4
UNROLL_A = 3
UNROLL_T = 8
UNROLL_S = 11
UNROLL_G = 4
TABLE_WIDTH = 512
GATHER_WIDTH = 1024
F32 = jnp.float32
BF16 = jnp.bfloat16
VMEM = pltpu.VMEM
WHOLE = pl.BlockSpec(memory_space=pltpu.VMEM)
SOMEWHERE = pl.BlockSpec(memory_space=pl.ANY)
HBM = pl.BlockSpec(memory_space=pltpu.HBM)


def params(mib):
    return pltpu.CompilerParams(vmem_limit_bytes=mib * 2**20)


def plane_rows(index, z):
    return pl.ds(pl.multiple_of((index * DEPTH + z) * ROWS, ROWS), ROWS)


def inverse_map(m0, m1, m2, u):
    if m0 is None and m1 is None and m2 is None:
        return None, None, None
    w = None if m0 is None else u * m0
    if m1 is not None:
        w = m1 if w is None else w + m1
    t = None
    if w is not None:
        t = u * (w if m1 is None else w + m1)
    if m2 is not None:
        t = m2 if t is None else t + m2
    if w is None:
        return t, -t, t
    return t - w, (-t if m0 is None else m0 - t), t + w


def collide(f):
    def at(a, b, c):
        return f[a * 9 + b * 3 + c]

    ends = [[at(a, b, 2) + at(a, b, 0) for b in range(3)] for a in range(3)]
    dz = [[at(a, b, 2) - at(a, b, 0) for b in range(3)] for a in range(3)]
    s = [[ends[a][b] + at(a, b, 1) for b in range(3)] for a in range(3)]
    row = [s[a][0] + s[a][1] + s[a][2] for a in range(3)]
    density = row[0] + row[1] + row[2]
    q0 = s[0][0] + s[1][0] + s[2][0]
    q2 = s[0][2] + s[1][2] + s[2][2]
    dzx = [dz[a][0] + dz[a][1] + dz[a][2] for a in range(3)]
    dzy0 = dz[0][0] + dz[1][0] + dz[2][0]
    dzy2 = dz[0][2] + dz[1][2] + dz[2][2]
    pzz = sum(ends[a][b] for a in range(3) for b in range(3))
    inv = 1.0 / density
    ux = (row[2] - row[0]) * inv
    uy = (q2 - q0) * inv
    uz = (dzx[0] + dzx[1] + dzx[2]) * inv
    keep = 1.0 - RELAXATION
    third = RELAXATION / 3.0

    def spread(p, first, second):
        return keep * (p * inv - first * second)

    xx = spread(row[2] + row[0], ux, ux) + third
    yy = spread(q2 + q0, uy, uy) + third
    zz = spread(pzz, uz, uz) + third
    xy = spread((s[2][2] - s[2][0]) + (s[0][0] - s[0][2]), ux, uy)
    xz = spread(dzx[2] - dzx[0], ux, uz)
    yz = spread(dzy2 - dzy0, uy, uz)
    xy2, xz2, yz2 = 2.0 * xy, 2.0 * xz, 2.0 * yz
    e220 = xx * yy + xy2 * xy
    e202 = xx * zz + xz2 * xz
    eyz = yy * zz + yz2 * yz
    e211 = xx * yz + xy2 * xz
    e121 = yy * xz + xy2 * yz
    e112 = zz * xy + xz2 * yz
    e222 = xx * eyz + xz2 * e121 + xy2 * e112
    k = {
        (0, 0, 0): jnp.ones_like(density),
        (2, 0, 0): xx,
        (0, 2, 0): yy,
        (0, 0, 2): zz,
        (1, 1, 0): xy,
        (1, 0, 1): xz,
        (0, 1, 1): yz,
        (2, 2, 0): e220,
        (2, 0, 2): e202,
        (0, 2, 2): eyz,
        (2, 1, 1): e211,
        (1, 2, 1): e121,
        (1, 1, 2): e112,
        (2, 2, 2): e222,
    }
    along_z, along_y, result = {}, {}, [None] * 27
    for a in range(3):
        for b in range(3):
            out = inverse_map(k.get((a, b, 0)), k.get((a, b, 1)), k.get((a, b, 2)), uz)
            for c in range(3):
                along_z[a, b, c] = out[c]
    for a in range(3):
        for c in range(3):
            out = inverse_map(along_z[a, 0, c], along_z[a, 1, c], along_z[a, 2, c], uy)
            for b in range(3):
                along_y[a, b, c] = out[b]
    scale = [density, 0.5 * density, 0.25 * density, 0.125 * density]
    for b in range(3):
        for c in range(3):
            out = inverse_map(along_y[0, b, c], along_y[1, b, c], along_y[2, b, c], ux)
            for a in range(3):
                moving = abs(a - 1) + abs(b - 1) + abs(c - 1)
                result[a * 9 + b * 3 + c] = scale[moving] * out[a]
    return result


def rim_kernel(pop_ref, buf_ref, near_ref, far_ref, stacked, turned, sem):
    even = lax.rem(lax.axis_index("gy"), 2) == 0
    step = DEPTH // CHUNKS
    copies = [
        pltpu.make_async_copy(
            pop_ref.at[:, pl.ds(i * step, step)], buf_ref.at[:, pl.ds(i * step, step)], sem.at[i]
        )
        for i in range(CHUNKS)
    ]
    for copy in copies:
        copy.start()
    stacked[...] = jnp.zeros_like(stacked)
    lane = lax.broadcasted_iota(jnp.int32, (ROWS, COLS), 1)
    packed = [None] * 27
    for z in range(DEPTH):
        if z % step == 0:
            copies[z // step].wait()
        here = lane // 2 == z
        for d in range(27):
            plane = pltpu.roll(buf_ref[d, z], 2 * z + 1, 1)
            packed[d] = plane if z == 0 else jnp.where(here, plane, packed[d])
    f = collide(packed)
    odd = lane % 2 == 1
    group = lane // 48
    for side in range(2):
        rim = []
        for v in range(3):
            value = jnp.zeros((ROWS, COLS), F32)
            for k in range(4 * v, min(4 * v + 4, 9)):
                d = k // 3 * 9 + k % 3 + (6 if side == 1 else 0)
                place = k % 4
                shift = (place // 2) * 48 + place % 2 - (0 if side == 1 else 1)
                moved = f[d] if shift == 0 else pltpu.roll(f[d], shift % COLS, 1)
                mine = (group == place // 2) & (odd == (place % 2 == 1))
                value = jnp.where(mine, moved, value)
            rim.append(value)
        for v in range(3):
            at = slice(v * ROWS, (v + 1) * ROWS)

            @pl.when(even == (side == 1))
            def _():
                near_ref[at, :] = rim[v]

            @pl.when(even != (side == 1))
            def _():
                far_ref[at, :] = rim[v]

        for end in range(2):
            for c in range(3):
                d = end * 18 + c + (6 if side == 1 else 0)
                x = end * (ROWS - 1)
                place = end * 3 + c + side * 8
                stacked[place : place + 1, :] = f[d][x : x + 1, :]
    turned[...] = stacked[...].T
    low = turned[pl.ds(1, DEPTH, stride=2), :]
    high = turned[pl.ds(0, DEPTH, stride=2), :]
    near_ref[DEPTH:, :] = jnp.where(even, high, low)
    far_ref[DEPTH:, :] = jnp.where(even, low, high)


def collide_kernel(buf_ref, col_ref):
    def body(z, carry):
        f = collide([buf_ref[d, z] for d in range(27)])
        for d in range(27):
            col_ref[plane_rows(d, z), :] = f[d]
        return carry

    lax.fori_loop(0, DEPTH, body, 0, unroll=UNROLL_A)


def edge_kernel(col_ref, near_ref, far_ref, pair_ref, other_ref):
    even = lax.rem(lax.axis_index("gy"), 2) == 0
    even_x = lax.rem(lax.axis_index("gx"), 2) == 0
    lane = lax.broadcasted_iota(jnp.int32, (DEPTH, COLS), 1)
    low = jnp.where(even, far_ref[DEPTH:, :], near_ref[DEPTH:, :])
    high = jnp.where(even, near_ref[DEPTH:, :], far_ref[DEPTH:, :])
    for end in range(2):
        rows = []
        for b in range(3):
            for c in range(3):
                start = (end * 18 + b * 3 + c) * PLANES + end * (ROWS - 1)
                row = col_ref[pl.ds(start, DEPTH, stride=ROWS), :]
                spot = end * 3 + c
                if b == 2:
                    halo = pltpu.roll(low, COLS - spot - 8, 1)
                    row = jnp.where(lane == 0, halo, pltpu.roll(row, 1, 1))
                elif b == 0:
                    halo = pltpu.roll(high, COLS - 1 - spot, 1)
                    row = jnp.where(lane == COLS - 1, halo, pltpu.roll(row, COLS - 1, 1))
                rows.append(row)

        @pl.when(even_x == (end == 1))
        def _():
            for k in range(9):
                pair_ref[k] = rows[k]

        @pl.when(even_x != (end == 1))
        def _():
            for k in range(9):
                other_ref[k] = rows[k]


def split_code(code):
    offset = jnp.where(code > 108.5, 2.0, jnp.where(code > 54.5, 1.0, 0.0))
    code = code - 54.0 * offset
    near = code > 27.5
    return offset, near, jnp.where(near, code - 28.0, code - 1.0)


def table_kernel(
    cell_ref, dir_ref, q_ref, panel_ref,
    dense_ref, row_ref, lane_ref, pan_ref, push_ref, late_push_ref, late_pan_ref,
    gathered,
):
    gx = lax.axis_index("gx")
    count = lax.axis_size("gx")
    per_row = PAN_DEV * lax.axis_size("gy")
    width = TABLE_WIDTH
    row_iota = lax.broadcasted_iota(jnp.int32, (PLANES, width), 0).astype(F32).astype(BF16)
    lane_iota = lax.broadcasted_iota(jnp.int32, (COLS, width), 0).astype(F32).astype(BF16)
    one, zero = jnp.ones((), BF16), jnp.zeros((), BF16)
    push_iota = lax.broadcasted_iota(jnp.int32, (24, width), 0)
    gathered[...] = jnp.zeros_like(gathered)

    def load(ref, i):
        n = width // COLS
        return jnp.concatenate([ref[pl.ds(n * i + j, 1), :] for j in range(n)], axis=1)

    def spread(value, count):
        tile = jnp.broadcast_to(value.astype(F32), (16, width)).astype(BF16)
        return jnp.concatenate([tile] * (count // 16), axis=0)

    def body(i, carry):
        at = pl.ds(pl.multiple_of(i * width, width), width)
        cell, direction = load(cell_ref, i), load(dir_ref, i)
        q, panel = load(q_ref, i), load(panel_ref, i)
        active = panel >= 0
        near = q < 0.5
        twice = 2.0 * q
        weight = jnp.where(near, twice, 1.0 / twice)
        weight_hi = weight.astype(BF16).astype(F32)
        weight_lo = weight - weight_hi
        offset = panel // per_row - gx + 1
        offset = jnp.where(offset < 0, offset + count, offset)
        offset = jnp.where(offset >= count, offset - count, offset)
        code = (direction + 1 + jnp.where(near, 27, 0) + 54 * offset).astype(F32)
        spot = panel % PAN_DEV
        row = jnp.where(active, cell // COLS, -1)
        rows = jnp.where(row_iota == spread(row, PLANES), one, zero)
        row_ref[:, at] = rows
        here = lane_iota == spread(cell % COLS, COLS)
        lane_ref[:, at] = jnp.where(here, one, zero)
        values = jnp.concatenate(
            [
                jnp.where(here, spread(v, COLS), zero)
                for v in (weight_hi, weight_lo, code, spot)
            ],
            axis=0,
        )
        gathered[...] += lax.dot_general(
            rows, values, (((1,), (1,)), ((), ())), preferred_element_type=F32
        )
        pan_ref[:, at] = jnp.where(lane_iota == spread(spot, PAN_DEV), one, zero)
        part = push_iota % 8
        step = jnp.where(
            part == 0,
            direction // 9 - 1,
            jnp.where(part == 1, direction // 3 % 3 - 1, direction % 3 - 1),
        )
        chosen = active & (push_iota // 8 == offset) & (part < 3)
        push_ref[:, at] = jnp.where(chosen, step, 0).astype(F32)
        return carry

    lax.fori_loop(0, LINKS // width, body, 0, unroll=UNROLL_T)
    dense_ref[:PLANES, :] = gathered[:, :COLS] + gathered[:, COLS : 2 * COLS]
    dense_ref[PLANES : 2 * PLANES, :] = gathered[:, 2 * COLS : 3 * COLS]
    dense_ref[2 * PLANES :, :] = gathered[:, 3 * COLS :]

    even_x = lax.rem(gx, 2) == 0
    last = jnp.where(even_x, 0, ROWS - 1)
    picked = [dense_ref[pl.ds(i * PLANES + last, DEPTH, stride=ROWS), :] for i in range(3)]
    offset, near, which = split_code(picked[1])
    lead = jnp.where(even_x, 18.0, 0.0)
    across = near & (which >= lead) & (which < lead + 9.0)
    share = jnp.where(across, 1.0 - picked[0], 0.0)
    k = jnp.where(across, which - lead, 0.0)
    step_y = jnp.where(k > 5.5, 1.0, jnp.where(k > 2.5, 0.0, -1.0))
    step_z = k - 3.0 * step_y - 4.0
    step_x = jnp.where(even_x, share, -share)
    step_y, step_z = step_y * share, step_z * share
    push_iota = lax.broadcasted_iota(jnp.int32, (24, COLS), 0)
    part, owner = push_iota % 8, (push_iota // 8).astype(F32)
    pan_iota = lax.broadcasted_iota(jnp.int32, (PAN_DEV, COLS), 0).astype(F32)
    for z in range(DEPTH):
        row = slice(z, z + 1)
        steps = jnp.where(
            part == 0,
            step_x[row],
            jnp.where(part == 1, step_y[row], jnp.where(part == 2, step_z[row], 0.0)),
        )
        at = slice(z * COLS, (z + 1) * COLS)
        late_push_ref[:, at] = jnp.where(owner == offset[row], steps, 0.0)
        late_pan_ref[:, at] = jnp.where(pan_iota == picked[2][row], 1.0, 0.0).astype(BF16)


def by_panel(push, pan):
    push_hi = push.astype(BF16).astype(F32)
    push = jnp.concatenate([push_hi, push - push_hi], axis=0).astype(BF16)
    return lax.dot_general(push, pan, (((1,), (1,)), ((), ())), preferred_element_type=F32)


def stream_kernel(
    col_ref, near_ref, far_ref, pair_ref, dense_ref, row_ref, lane_ref, pan_ref, push_ref, mask_ref,
    new_ref, force_ref,
    edges, halo, momentum,
):
    even = lax.rem(lax.axis_index("gy"), 2) == 0
    even_x = lax.rem(lax.axis_index("gx"), 2) == 0
    halo[0] = jnp.where(even_x, 0.0, pair_ref[...])
    halo[1] = jnp.where(even_x, pair_ref[...], 0.0)
    edges[0] = jnp.where(even, far_ref[:DEPTH, :], near_ref[:DEPTH, :])
    edges[1] = jnp.where(even, near_ref[:DEPTH, :], far_ref[:DEPTH, :])
    sub = lax.broadcasted_iota(jnp.int32, (ROWS, COLS), 0)
    lane = lax.broadcasted_iota(jnp.int32, (ROWS, COLS), 1)

    def body(z, bottom, top):
        here_rows = pl.ds(pl.multiple_of(z * ROWS, ROWS), ROWS)
        code = dense_ref[pl.ds(pl.multiple_of(PLANES + z * ROWS, ROWS), ROWS), :]
        weight = dense_ref[here_rows, :]
        fluid = (1 - mask_ref[z]).astype(F32)
        offset, near, which = split_code(code)
        toward = jnp.zeros((ROWS, COLS), F32)
        second, reverse = toward, toward
        for d in range(27):
            a, b, c = d // 9, d // 3 % 3, d % 3
            here = col_ref[plane_rows(d, z), :]
            back = col_ref[plane_rows(26 - d, z), :]
            if (c == 2 and bottom) or (c == 0 and top):
                moved = back
            else:
                zs = z - (c - 1)
                moved = col_ref[plane_rows(d, zs), :]
                k = a * 3 + c
                spot = 2 * zs + k % 4 // 2 * 48 + k % 2
                at = slice(k // 4 * ROWS, k // 4 * ROWS + ROWS)
                if b == 2:
                    side = pltpu.roll(edges[0, at, :], COLS - spot, 1)
                    moved = jnp.where(lane == 0, side, pltpu.roll(moved, 1, 1))
                elif b == 0:
                    side = pltpu.roll(edges[1, at, :], COLS - 1 - spot, 1)
                    moved = jnp.where(lane == COLS - 1, side, pltpu.roll(moved, COLS - 1, 1))
                if a == 2:
                    edge = halo[0, b * 3 + c, pl.ds(zs, 1), :]
                    moved = jnp.where(sub == 0, edge, pltpu.roll(moved, 1, 0))
                elif a == 0:
                    edge = halo[1, b * 3 + c, pl.ds(zs, 1), :]
                    moved = jnp.where(sub == ROWS - 1, edge, pltpu.roll(moved, ROWS - 1, 0))
            new_ref[plane_rows(d, z), :] = moved
            if d != 13:
                match = which == float(d)
                toward = jnp.where(match, here, toward)
                second = jnp.where(match, moved, second)
                reverse = jnp.where(match, back, reverse)
        other = jnp.where(near, second, reverse)
        bounce = other + weight * (toward - other)
        momentum[here_rows, :] = jnp.where(code > 0.5, toward + bounce, 0.0)
        for d in range(27):
            value = new_ref[plane_rows(d, z), :]
            if d != 13:
                value = jnp.where(which == float(26 - d), bounce, value)
            new_ref[plane_rows(d, z), :] = value * fluid

    body(0, True, False)
    lax.fori_loop(
        1, DEPTH - 1, lambda z, carry: (body(z, False, False), carry)[1], 0, unroll=UNROLL_S
    )
    body(DEPTH - 1, False, True)

    turned = momentum[...].T
    turned_hi = turned.astype(BF16)
    turned_lo = (turned - turned_hi.astype(F32)).astype(BF16)
    width = GATHER_WIDTH

    def gather(i, total):
        at = pl.ds(pl.multiple_of(i * width, width), width)
        rows = row_ref[:, at]
        picked = jnp.dot(turned_hi, rows, preferred_element_type=F32) + jnp.dot(
            turned_lo, rows, preferred_element_type=F32
        )
        value = jnp.sum(picked * lane_ref[:, at].astype(F32), axis=0, keepdims=True)
        return total + by_panel(push_ref[:, at] * value, pan_ref[:, at])

    total = lax.fori_loop(
        0, LINKS // width, gather, jnp.zeros((48, PAN_DEV), F32), unroll=UNROLL_G
    )
    force_ref[...] = total[:24] + total[24:]


def late_row(dense_ref, even_x):
    last = jnp.where(even_x, 0, ROWS - 1)
    weight = dense_ref[pl.ds(last, DEPTH, stride=ROWS), :]
    _, near, which = split_code(dense_ref[pl.ds(PLANES + last, DEPTH, stride=ROWS), :])
    return near, which, weight


def late_kernel(other_ref, dense_ref, force_ref, late_push_ref, late_pan_ref, own_ref, send_pair_ref, send_other_ref):
    even_x = lax.rem(lax.axis_index("gx"), 2) == 0
    near, which, weight = late_row(dense_ref, even_x)
    lead = jnp.where(even_x, 18.0, 0.0)
    second = jnp.zeros((DEPTH, COLS), F32)
    for k in range(9):
        row = other_ref[k]
        if k % 3 == 2:
            row = pltpu.roll(row, 1, 0)
        elif k % 3 == 0:
            row = pltpu.roll(row, DEPTH - 1, 0)
        second = jnp.where(which == lead + float(k), row, second)
    second = jnp.concatenate([second[z : z + 1] for z in range(DEPTH)], axis=1)
    late = by_panel(late_push_ref[...] * second, late_pan_ref[...])
    force = force_ref[...] + late[:24] + late[24:]
    own_ref[...] = force[8:16]
    send_pair_ref[...] = jnp.where(even_x, force[16:24], force[0:8])
    send_other_ref[...] = jnp.where(even_x, force[0:8], force[16:24])


def finish_kernel(new_in_ref, other_ref, dense_ref, mask_ref, out_ref, new_ref, sem):
    del new_in_ref
    even_x = lax.rem(lax.axis_index("gx"), 2) == 0
    near, which, weight = late_row(dense_ref, even_x)
    last = jnp.where(even_x, 0, ROWS - 1)
    lead_index = jnp.where(even_x, 18, 0)
    lead = lead_index.astype(F32)
    fluid = (1 - mask_ref[pl.ds(last, DEPTH, stride=ROWS), :]).astype(F32)
    level = lax.broadcasted_iota(jnp.int32, (DEPTH, COLS), 0)
    for k in range(9):
        row = other_ref[k]
        inside = level >= 0
        if k % 3 == 2:
            row = pltpu.roll(row, 1, 0)
            inside = level > 0
        elif k % 3 == 0:
            row = pltpu.roll(row, DEPTH - 1, 0)
            inside = level < DEPTH - 1
        row = row * fluid
        index = lead_index + k
        at = pl.ds(index * PLANES + last, DEPTH, stride=ROWS)
        free = inside & (which != 26.0 - lead - float(k))
        new_ref[at, :] = jnp.where(free, row, new_ref[at, :])
        at = pl.ds((26 - index) * PLANES + last, DEPTH, stride=ROWS)
        hit = near & (which == lead + float(k))
        new_ref[at, :] = new_ref[at, :] + jnp.where(hit, (1.0 - weight) * row, 0.0)
    copy = pltpu.make_async_copy(new_ref, out_ref, sem)
    copy.start()
    copy.wait()


def pair_swap(count):
    return [(i, i ^ 1) for i in range(count)]


def other_swap(count):
    return [(i, (i + 1) % count if i % 2 else (i - 1) % count) for i in range(count)]


def per_device(populations, solid_mask, link_cell, link_dir, link_second, link_q, link_panel):
    nx, ny = lax.axis_size("gx"), lax.axis_size("gy")
    small = jax.ShapeDtypeStruct((ROWS, PAN_DEV), F32)
    column = jax.ShapeDtypeStruct((2 * DEPTH, COLS), F32)
    edge = jax.ShapeDtypeStruct((9, DEPTH, COLS), F32)
    arrived, y_pair, y_other = pl.pallas_call(
        rim_kernel,
        out_shape=(VMEM(populations.shape, F32), column, column),
        in_specs=[HBM],
        scratch_shapes=[
            VMEM((COLS, COLS), F32),
            VMEM((COLS, COLS), F32),
            pltpu.SemaphoreType.DMA((CHUNKS,)),
        ],
        compiler_params=params(16),
        name="rims",
    )(pltpu.with_memory_space_constraint(populations, pltpu.HBM))
    y_other = lax.ppermute(y_other, "gy", other_swap(ny))
    y_pair = lax.ppermute(y_pair, "gy", pair_swap(ny))
    collided = pl.pallas_call(
        collide_kernel,
        out_shape=VMEM((27 * PLANES, COLS), F32),
        in_specs=[WHOLE],
        compiler_params=params(16),
        cost_estimate=pl.CostEstimate(flops=10**9, bytes_accessed=5 * 10**6, transcendentals=0),
        name="collide",
    )(arrived)
    x_pair, x_other = pl.pallas_call(
        edge_kernel,
        out_shape=(edge, edge),
        in_specs=[WHOLE] * 3,
        compiler_params=params(16),
        name="edges",
    )(collided, y_pair, y_other)
    x_other = lax.ppermute(x_other, "gx", other_swap(nx))
    x_pair = lax.ppermute(x_pair, "gx", pair_swap(nx))
    tables = [t.reshape(LINKS // COLS, COLS) for t in (link_cell, link_dir, link_q, link_panel)]
    tables = pl.pallas_call(
        table_kernel,
        out_shape=(
            VMEM((3 * PLANES, COLS), F32),
            VMEM((PLANES, LINKS), BF16),
            VMEM((COLS, LINKS), BF16),
            VMEM((PAN_DEV, LINKS), BF16),
            VMEM((24, LINKS), F32),
            VMEM((24, DEPTH * COLS), F32),
            VMEM((PAN_DEV, DEPTH * COLS), BF16),
        ),
        in_specs=[WHOLE] * 4,
        scratch_shapes=[VMEM((PLANES, 4 * COLS), F32)],
        compiler_params=params(16),
        cost_estimate=pl.CostEstimate(flops=6 * 10**9, bytes_accessed=70000, transcendentals=0),
        name="tables",
    )(*tables)
    *tables, late_push, late_pan = tables
    dense = tables[0]
    moved, force = pl.pallas_call(
        stream_kernel,
        out_shape=(
            VMEM((27 * PLANES, COLS), F32),
            VMEM((24, PAN_DEV), F32),
        ),
        in_specs=[WHOLE] * 10,
        scratch_shapes=[
            VMEM((2, DEPTH, COLS), F32),
            VMEM((2, 9, DEPTH, COLS), F32),
            VMEM((PLANES, COLS), F32),
        ],
        compiler_params=params(24),
        name="stream",
    )(collided, y_pair, y_other, x_pair, *tables, solid_mask)
    own, to_pair, to_other = pl.pallas_call(
        late_kernel,
        out_shape=(small, small, small),
        in_specs=[WHOLE] * 5,
        compiler_params=params(16),
        name="late",
    )(x_other, dense, force, late_push, late_pan)
    from_other = lax.ppermute(to_other, "gx", other_swap(nx))
    from_pair = lax.ppermute(to_pair, "gx", pair_swap(nx))
    populations_next, _ = pl.pallas_call(
        finish_kernel,
        out_shape=(
            jax.ShapeDtypeStruct((27 * PLANES, COLS), F32),
            VMEM((27 * PLANES, COLS), F32),
        ),
        in_specs=[WHOLE] * 4,
        out_specs=(SOMEWHERE, WHOLE),
        input_output_aliases={0: 1},
        scratch_shapes=[pltpu.SemaphoreType.DMA],
        compiler_params=params(16),
        name="finish",
    )(moved, x_other, dense, solid_mask.reshape(PLANES, COLS))
    return populations_next.reshape(populations.shape), (own + from_pair + from_other)[:3]


def solution(mesh):
    return jax.shard_map(
        per_device,
        mesh=mesh,
        in_specs=(
            P(None, None, "gx", "gy"),
            P(None, "gx", "gy"),
            P(("gx", "gy")),
            P(("gx", "gy")),
            P(("gx", "gy")),
            P(("gx", "gy")),
            P(("gx", "gy")),
        ),
        out_specs=(P(None, None, "gx", "gy"), P(None, ("gx", "gy"))),
        check_vma=False,
    )
```

```python
import functools

import jax
import jax.numpy as jnp
from jax import lax
from jax.experimental import pallas as pl
from jax.experimental.pallas import tpu as pltpu
from jax.sharding import PartitionSpec as P

PAN_DEV = 128
RELAXATION = 1.7
DEPTH, ROWS, COLS = 24, 8, 128
PLANES = DEPTH * ROWS
LINKS = 4096
HALF = DEPTH // 2
CHUNKS = 4
UNROLL_A = 3
UNROLL_T = 8
UNROLL_S = 11
UNROLL_G = 1
UNROLL_F = 8
TABLE_WIDTH = 512
GATHER_WIDTH = 4096
F32 = jnp.float32
BF16 = jnp.bfloat16
VMEM = pltpu.VMEM
WHOLE = pl.BlockSpec(memory_space=pltpu.VMEM)
SOMEWHERE = pl.BlockSpec(memory_space=pl.ANY)
HBM = pl.BlockSpec(memory_space=pltpu.HBM)


def params(mib):
    return pltpu.CompilerParams(vmem_limit_bytes=mib * 2**20)


def plane_rows(index, z):
    return pl.ds(pl.multiple_of((index * DEPTH + z) * ROWS, ROWS), ROWS)


def inverse_map(m0, m1, m2, u):
    if m0 is None and m1 is None and m2 is None:
        return None, None, None
    w = None if m0 is None else u * m0
    if m1 is not None:
        w = m1 if w is None else w + m1
    t = None
    if w is not None:
        t = u * (w if m1 is None else w + m1)
    if m2 is not None:
        t = m2 if t is None else t + m2
    if w is None:
        return t, -t, t
    return t - w, (-t if m0 is None else m0 - t), t + w


def collide(f):
    def at(a, b, c):
        return f[a * 9 + b * 3 + c]

    ends = [[at(a, b, 2) + at(a, b, 0) for b in range(3)] for a in range(3)]
    dz = [[at(a, b, 2) - at(a, b, 0) for b in range(3)] for a in range(3)]
    s = [[ends[a][b] + at(a, b, 1) for b in range(3)] for a in range(3)]
    row = [s[a][0] + s[a][1] + s[a][2] for a in range(3)]
    density = row[0] + row[1] + row[2]
    q0 = s[0][0] + s[1][0] + s[2][0]
    q2 = s[0][2] + s[1][2] + s[2][2]
    dzx = [dz[a][0] + dz[a][1] + dz[a][2] for a in range(3)]
    dzy0 = dz[0][0] + dz[1][0] + dz[2][0]
    dzy2 = dz[0][2] + dz[1][2] + dz[2][2]
    pzz = sum(ends[a][b] for a in range(3) for b in range(3))
    inv = 1.0 / density
    ux = (row[2] - row[0]) * inv
    uy = (q2 - q0) * inv
    uz = (dzx[0] + dzx[1] + dzx[2]) * inv
    keep = 1.0 - RELAXATION
    third = RELAXATION / 3.0

    def spread(p, first, second):
        return keep * (p * inv - first * second)

    xx = spread(row[2] + row[0], ux, ux) + third
    yy = spread(q2 + q0, uy, uy) + third
    zz = spread(pzz, uz, uz) + third
    xy = spread((s[2][2] - s[2][0]) + (s[0][0] - s[0][2]), ux, uy)
    xz = spread(dzx[2] - dzx[0], ux, uz)
    yz = spread(dzy2 - dzy0, uy, uz)
    xy2, xz2, yz2 = 2.0 * xy, 2.0 * xz, 2.0 * yz
    e220 = xx * yy + xy2 * xy
    e202 = xx * zz + xz2 * xz
    eyz = yy * zz + yz2 * yz
    e211 = xx * yz + xy2 * xz
    e121 = yy * xz + xy2 * yz
    e112 = zz * xy + xz2 * yz
    e222 = xx * eyz + xz2 * e121 + xy2 * e112
    k = {
        (0, 0, 0): jnp.ones_like(density),
        (2, 0, 0): xx,
        (0, 2, 0): yy,
        (0, 0, 2): zz,
        (1, 1, 0): xy,
        (1, 0, 1): xz,
        (0, 1, 1): yz,
        (2, 2, 0): e220,
        (2, 0, 2): e202,
        (0, 2, 2): eyz,
        (2, 1, 1): e211,
        (1, 2, 1): e121,
        (1, 1, 2): e112,
        (2, 2, 2): e222,
    }
    along_z, along_y, result = {}, {}, [None] * 27
    for a in range(3):
        for b in range(3):
            out = inverse_map(k.get((a, b, 0)), k.get((a, b, 1)), k.get((a, b, 2)), uz)
            for c in range(3):
                along_z[a, b, c] = out[c]
    for a in range(3):
        for c in range(3):
            out = inverse_map(along_z[a, 0, c], along_z[a, 1, c], along_z[a, 2, c], uy)
            for b in range(3):
                along_y[a, b, c] = out[b]
    scale = [density, 0.5 * density, 0.25 * density, 0.125 * density]
    for b in range(3):
        for c in range(3):
            out = inverse_map(along_y[0, b, c], along_y[1, b, c], along_y[2, b, c], ux)
            for a in range(3):
                moving = abs(a - 1) + abs(b - 1) + abs(c - 1)
                result[a * 9 + b * 3 + c] = scale[moving] * out[a]
    return result


def rim_kernel(pop_ref, buf_ref, near_ref, far_ref, stacked, turned, sem):
    even = lax.rem(lax.axis_index("gy"), 2) == 0
    step = DEPTH // CHUNKS
    copies = [
        pltpu.make_async_copy(
            pop_ref.at[:, pl.ds(i * step, step)], buf_ref.at[:, pl.ds(i * step, step)], sem.at[i]
        )
        for i in range(CHUNKS)
    ]
    for copy in copies:
        copy.start()
    stacked[...] = jnp.zeros_like(stacked)
    lane = lax.broadcasted_iota(jnp.int32, (ROWS, COLS), 1)
    packed = [None] * 27
    for z in range(DEPTH):
        if z % step == 0:
            copies[z // step].wait()
        here = lane // 2 == z
        for d in range(27):
            plane = pltpu.roll(buf_ref[d, z], 2 * z + 1, 1)
            packed[d] = plane if z == 0 else jnp.where(here, plane, packed[d])
    f = collide(packed)
    odd = lane % 2 == 1
    group = lane // 48
    for side in range(2):
        rim = []
        for v in range(3):
            value = jnp.zeros((ROWS, COLS), F32)
            for k in range(4 * v, min(4 * v + 4, 9)):
                d = k // 3 * 9 + k % 3 + (6 if side == 1 else 0)
                place = k % 4
                shift = (place // 2) * 48 + place % 2 - (0 if side == 1 else 1)
                moved = f[d] if shift == 0 else pltpu.roll(f[d], shift % COLS, 1)
                mine = (group == place // 2) & (odd == (place % 2 == 1))
                value = jnp.where(mine, moved, value)
            rim.append(value)
        for v in range(3):
            at = slice(v * ROWS, (v + 1) * ROWS)

            @pl.when(even == (side == 1))
            def _():
                near_ref[at, :] = rim[v]

            @pl.when(even != (side == 1))
            def _():
                far_ref[at, :] = rim[v]

        for end in range(2):
            for c in range(3):
                d = end * 18 + c + (6 if side == 1 else 0)
                x = end * (ROWS - 1)
                place = end * 3 + c + side * 8
                stacked[place : place + 1, :] = f[d][x : x + 1, :]
    turned[...] = stacked[...].T
    low = turned[pl.ds(1, DEPTH, stride=2), :]
    high = turned[pl.ds(0, DEPTH, stride=2), :]
    near_ref[DEPTH:, :] = jnp.where(even, high, low)
    far_ref[DEPTH:, :] = jnp.where(even, low, high)


def collide_kernel(buf_ref, col_ref):
    def body(z, carry):
        f = collide([buf_ref[d, z] for d in range(27)])
        for d in range(27):
            col_ref[plane_rows(d, z), :] = f[d]
        return carry

    lax.fori_loop(0, DEPTH, body, 0, unroll=UNROLL_A)


def edge_kernel(col_ref, near_ref, far_ref, pair_ref, other_ref):
    even = lax.rem(lax.axis_index("gy"), 2) == 0
    even_x = lax.rem(lax.axis_index("gx"), 2) == 0
    lane = lax.broadcasted_iota(jnp.int32, (DEPTH, COLS), 1)
    low = jnp.where(even, far_ref[DEPTH:, :], near_ref[DEPTH:, :])
    high = jnp.where(even, near_ref[DEPTH:, :], far_ref[DEPTH:, :])
    for end in range(2):
        rows = []
        for b in range(3):
            for c in range(3):
                start = (end * 18 + b * 3 + c) * PLANES + end * (ROWS - 1)
                row = col_ref[pl.ds(start, DEPTH, stride=ROWS), :]
                spot = end * 3 + c
                if b == 2:
                    halo = pltpu.roll(low, COLS - spot - 8, 1)
                    row = jnp.where(lane == 0, halo, pltpu.roll(row, 1, 1))
                elif b == 0:
                    halo = pltpu.roll(high, COLS - 1 - spot, 1)
                    row = jnp.where(lane == COLS - 1, halo, pltpu.roll(row, COLS - 1, 1))
                rows.append(row)

        @pl.when(even_x == (end == 1))
        def _():
            for k in range(9):
                pair_ref[k] = rows[k]

        @pl.when(even_x != (end == 1))
        def _():
            for k in range(9):
                other_ref[k] = rows[k]


def split_code(code):
    offset = jnp.where(code > 108.5, 2.0, jnp.where(code > 54.5, 1.0, 0.0))
    code = code - 54.0 * offset
    near = code > 27.5
    return offset, near, jnp.where(near, code - 28.0, code - 1.0)


def table_kernel(
    cell_ref, dir_ref, q_ref, panel_ref,
    dense_ref, row_ref, lane_ref, pan_ref, push_ref, late_push_ref, late_pan_ref,
    gathered,
):
    gx = lax.axis_index("gx")
    count = lax.axis_size("gx")
    per_row = PAN_DEV * lax.axis_size("gy")
    width = TABLE_WIDTH
    row_iota = lax.broadcasted_iota(jnp.int32, (PLANES, width), 0).astype(F32).astype(BF16)
    lane_iota = lax.broadcasted_iota(jnp.int32, (COLS, width), 0).astype(F32).astype(BF16)
    one, zero = jnp.ones((), BF16), jnp.zeros((), BF16)
    push_iota = lax.broadcasted_iota(jnp.int32, (24, width), 0)
    gathered[...] = jnp.zeros_like(gathered)

    def load(ref, i):
        n = width // COLS
        return jnp.concatenate([ref[pl.ds(n * i + j, 1), :] for j in range(n)], axis=1)

    def spread(value, count):
        tile = jnp.broadcast_to(value.astype(F32), (16, width)).astype(BF16)
        return jnp.concatenate([tile] * (count // 16), axis=0)

    def body(i, carry):
        at = pl.ds(pl.multiple_of(i * width, width), width)
        cell, direction = load(cell_ref, i), load(dir_ref, i)
        q, panel = load(q_ref, i), load(panel_ref, i)
        active = panel >= 0
        near = q < 0.5
        twice = 2.0 * q
        weight = jnp.where(near, twice, 1.0 / twice)
        weight_hi = weight.astype(BF16).astype(F32)
        weight_lo = weight - weight_hi
        offset = panel // per_row - gx + 1
        offset = jnp.where(offset < 0, offset + count, offset)
        offset = jnp.where(offset >= count, offset - count, offset)
        code = (direction + 1 + jnp.where(near, 27, 0) + 54 * offset).astype(F32)
        spot = panel % PAN_DEV
        row = jnp.where(active, cell // COLS, -1)
        rows = jnp.where(row_iota == spread(row, PLANES), one, zero)
        row_ref[:, at] = rows
        here = lane_iota == spread(cell % COLS, COLS)
        lane_ref[:, at] = jnp.where(here, one, zero)
        values = jnp.concatenate(
            [
                jnp.where(here, spread(v, COLS), zero)
                for v in (weight_hi, weight_lo, code, spot)
            ],
            axis=0,
        )
        gathered[...] += lax.dot_general(
            rows, values, (((1,), (1,)), ((), ())), preferred_element_type=F32
        )
        pan_ref[:, at] = jnp.where(lane_iota == spread(spot, PAN_DEV), one, zero)
        part = push_iota % 8
        step = jnp.where(
            part == 0,
            direction // 9 - 1,
            jnp.where(part == 1, direction // 3 % 3 - 1, direction % 3 - 1),
        )
        chosen = active & (push_iota // 8 == offset) & (part < 3)
        push_ref[:, at] = jnp.where(chosen, step, 0).astype(F32)
        return carry

    lax.fori_loop(0, LINKS // width, body, 0, unroll=UNROLL_T)
    dense_ref[:PLANES, :] = gathered[:, :COLS] + gathered[:, COLS : 2 * COLS]
    dense_ref[PLANES : 2 * PLANES, :] = gathered[:, 2 * COLS : 3 * COLS]
    dense_ref[2 * PLANES :, :] = gathered[:, 3 * COLS :]

    even_x = lax.rem(gx, 2) == 0
    last = jnp.where(even_x, 0, ROWS - 1)
    picked = [dense_ref[pl.ds(i * PLANES + last, DEPTH, stride=ROWS), :] for i in range(3)]
    offset, near, which = split_code(picked[1])
    lead = jnp.where(even_x, 18.0, 0.0)
    across = near & (which >= lead) & (which < lead + 9.0)
    share = jnp.where(across, 1.0 - picked[0], 0.0)
    k = jnp.where(across, which - lead, 0.0)
    step_y = jnp.where(k > 5.5, 1.0, jnp.where(k > 2.5, 0.0, -1.0))
    step_z = k - 3.0 * step_y - 4.0
    step_x = jnp.where(even_x, share, -share)
    step_y, step_z = step_y * share, step_z * share
    push_iota = lax.broadcasted_iota(jnp.int32, (24, COLS), 0)
    part, owner = push_iota % 8, (push_iota // 8).astype(F32)
    pan_iota = lax.broadcasted_iota(jnp.int32, (PAN_DEV, COLS), 0).astype(F32)
    for z in range(DEPTH):
        row = slice(z, z + 1)
        steps = jnp.where(
            part == 0,
            step_x[row],
            jnp.where(part == 1, step_y[row], jnp.where(part == 2, step_z[row], 0.0)),
        )
        at = slice(z * COLS, (z + 1) * COLS)
        late_push_ref[:, at] = jnp.where(owner == offset[row], steps, 0.0)
        late_pan_ref[:, at] = jnp.where(pan_iota == picked[2][row], 1.0, 0.0).astype(BF16)


def by_panel(push, pan):
    push_hi = push.astype(BF16).astype(F32)
    push = jnp.concatenate([push_hi, push - push_hi], axis=0).astype(BF16)
    return lax.dot_general(push, pan, (((1,), (1,)), ((), ())), preferred_element_type=F32)


def stream_kernel(
    col_ref, near_ref, far_ref, pair_ref, dense_ref, row_ref, lane_ref, pan_ref, push_ref,
    new_ref, bounce_ref, force_ref,
    edges, halo, momentum,
):
    even = lax.rem(lax.axis_index("gy"), 2) == 0
    even_x = lax.rem(lax.axis_index("gx"), 2) == 0
    halo[0] = jnp.where(even_x, 0.0, pair_ref[...])
    halo[1] = jnp.where(even_x, pair_ref[...], 0.0)
    edges[0] = jnp.where(even, far_ref[:DEPTH, :], near_ref[:DEPTH, :])
    edges[1] = jnp.where(even, near_ref[:DEPTH, :], far_ref[:DEPTH, :])
    sub = lax.broadcasted_iota(jnp.int32, (ROWS, COLS), 0)
    lane = lax.broadcasted_iota(jnp.int32, (ROWS, COLS), 1)

    def body(z, bottom, top):
        here_rows = pl.ds(pl.multiple_of(z * ROWS, ROWS), ROWS)
        code = dense_ref[pl.ds(pl.multiple_of(PLANES + z * ROWS, ROWS), ROWS), :]
        weight = dense_ref[here_rows, :]
        _, near, which = split_code(code)
        toward = jnp.zeros((ROWS, COLS), F32)
        second, reverse = toward, toward
        for d in range(27):
            a, b, c = d // 9, d // 3 % 3, d % 3
            here = col_ref[plane_rows(d, z), :]
            back = col_ref[plane_rows(26 - d, z), :]
            if (c == 2 and bottom) or (c == 0 and top):
                moved = back
            else:
                zs = z - (c - 1)
                moved = col_ref[plane_rows(d, zs), :]
                k = a * 3 + c
                spot = 2 * zs + k % 4 // 2 * 48 + k % 2
                at = slice(k // 4 * ROWS, k // 4 * ROWS + ROWS)
                if b == 2:
                    side = pltpu.roll(edges[0, at, :], COLS - spot, 1)
                    moved = jnp.where(lane == 0, side, pltpu.roll(moved, 1, 1))
                elif b == 0:
                    side = pltpu.roll(edges[1, at, :], COLS - 1 - spot, 1)
                    moved = jnp.where(lane == COLS - 1, side, pltpu.roll(moved, COLS - 1, 1))
                if a == 2:
                    edge = halo[0, b * 3 + c, pl.ds(zs, 1), :]
                    moved = jnp.where(sub == 0, edge, pltpu.roll(moved, 1, 0))
                elif a == 0:
                    edge = halo[1, b * 3 + c, pl.ds(zs, 1), :]
                    moved = jnp.where(sub == ROWS - 1, edge, pltpu.roll(moved, ROWS - 1, 0))
            new_ref[plane_rows(d, z), :] = moved
            if d != 13:
                match = which == float(d)
                toward = jnp.where(match, here, toward)
                second = jnp.where(match, moved, second)
                reverse = jnp.where(match, back, reverse)
        other = jnp.where(near, second, reverse)
        bounce = other + weight * (toward - other)
        momentum[here_rows, :] = jnp.where(code > 0.5, toward + bounce, 0.0)
        bounce_ref[here_rows, :] = bounce

    body(0, True, False)
    lax.fori_loop(
        1, DEPTH - 1, lambda z, carry: (body(z, False, False), carry)[1], 0, unroll=UNROLL_S
    )
    body(DEPTH - 1, False, True)

    turned = momentum[...].T
    turned_hi = turned.astype(BF16).astype(F32)
    turned = jnp.concatenate([turned_hi, turned - turned_hi], axis=0).astype(BF16)
    width = GATHER_WIDTH

    def gather(i, total):
        at = pl.ds(pl.multiple_of(i * width, width), width)
        rows = row_ref[:, at]
        picked = jnp.dot(turned, rows, preferred_element_type=F32)
        picked = picked[:COLS] + picked[COLS:]
        value = jnp.sum(picked * lane_ref[:, at].astype(F32), axis=0, keepdims=True)
        return total + by_panel(push_ref[:, at] * value, pan_ref[:, at])

    total = lax.fori_loop(
        0, LINKS // width, gather, jnp.zeros((48, PAN_DEV), F32), unroll=UNROLL_G
    )
    force_ref[...] = total[:24] + total[24:]


def late_row(dense_ref, even_x):
    last = jnp.where(even_x, 0, ROWS - 1)
    weight = dense_ref[pl.ds(last, DEPTH, stride=ROWS), :]
    _, near, which = split_code(dense_ref[pl.ds(PLANES + last, DEPTH, stride=ROWS), :])
    return near, which, weight


def late_kernel(other_ref, dense_ref, force_ref, late_push_ref, late_pan_ref, own_ref, send_pair_ref, send_other_ref):
    even_x = lax.rem(lax.axis_index("gx"), 2) == 0
    near, which, weight = late_row(dense_ref, even_x)
    lead = jnp.where(even_x, 18.0, 0.0)
    second = jnp.zeros((DEPTH, COLS), F32)
    for k in range(9):
        row = other_ref[k]
        if k % 3 == 2:
            row = pltpu.roll(row, 1, 0)
        elif k % 3 == 0:
            row = pltpu.roll(row, DEPTH - 1, 0)
        second = jnp.where(which == lead + float(k), row, second)
    second = jnp.concatenate([second[z : z + 1] for z in range(DEPTH)], axis=1)
    late = by_panel(late_push_ref[...] * second, late_pan_ref[...])
    force = force_ref[...] + late[:24] + late[24:]
    own_ref[...] = force[8:16]
    send_pair_ref[...] = jnp.where(even_x, force[16:24], force[0:8])
    send_other_ref[...] = jnp.where(even_x, force[0:8], force[16:24])


def finish_kernel(
    new_in_ref, bounce_in_ref, other_ref, dense_ref, mask_ref, out_ref, new_ref, bounce_ref, sem
):
    del new_in_ref, bounce_in_ref
    even_x = lax.rem(lax.axis_index("gx"), 2) == 0
    near, which, weight = late_row(dense_ref, even_x)
    last = jnp.where(even_x, 0, ROWS - 1)
    lead_index = jnp.where(even_x, 18, 0)
    lead = lead_index.astype(F32)
    level = lax.broadcasted_iota(jnp.int32, (DEPTH, COLS), 0)
    second = jnp.zeros((DEPTH, COLS), F32)
    for k in range(9):
        row = other_ref[k]
        at = pl.ds((lead_index + k) * PLANES + last, DEPTH, stride=ROWS)
        if k % 3 == 1:
            new_ref[at, :] = row
        else:
            row = pltpu.roll(row, 1 if k % 3 == 2 else DEPTH - 1, 0)
            inside = level > 0 if k % 3 == 2 else level < DEPTH - 1
            new_ref[at, :] = jnp.where(inside, row, new_ref[at, :])
        second = jnp.where(near & (which == lead + float(k)), row, second)
    at = pl.ds(last, DEPTH, stride=ROWS)
    bounce_ref[at, :] = bounce_ref[at, :] + (1.0 - weight) * second

    def body(z, carry):
        here_rows = pl.ds(pl.multiple_of(z * ROWS, ROWS), ROWS)
        _, _, target = split_code(dense_ref[pl.ds(pl.multiple_of(PLANES + z * ROWS, ROWS), ROWS), :])
        bounce = bounce_ref[here_rows, :]
        fluid = (1 - mask_ref[here_rows, :]).astype(F32)
        for d in range(27):
            value = new_ref[plane_rows(d, z), :]
            if d != 13:
                value = jnp.where(target == float(26 - d), bounce, value)
            new_ref[plane_rows(d, z), :] = value * fluid
        return carry

    lax.fori_loop(0, DEPTH, body, 0, unroll=UNROLL_F)
    copy = pltpu.make_async_copy(new_ref, out_ref, sem)
    copy.start()
    copy.wait()


def pair_swap(count):
    return [(i, i ^ 1) for i in range(count)]


def other_swap(count):
    return [(i, (i + 1) % count if i % 2 else (i - 1) % count) for i in range(count)]


def per_device(populations, solid_mask, link_cell, link_dir, link_second, link_q, link_panel):
    nx, ny = lax.axis_size("gx"), lax.axis_size("gy")
    small = jax.ShapeDtypeStruct((ROWS, PAN_DEV), F32)
    column = jax.ShapeDtypeStruct((2 * DEPTH, COLS), F32)
    edge = jax.ShapeDtypeStruct((9, DEPTH, COLS), F32)
    arrived, y_pair, y_other = pl.pallas_call(
        rim_kernel,
        out_shape=(VMEM(populations.shape, F32), column, column),
        in_specs=[HBM],
        scratch_shapes=[
            VMEM((COLS, COLS), F32),
            VMEM((COLS, COLS), F32),
            pltpu.SemaphoreType.DMA((CHUNKS,)),
        ],
        compiler_params=params(16),
        name="rims",
    )(pltpu.with_memory_space_constraint(populations, pltpu.HBM))
    y_other = lax.ppermute(y_other, "gy", other_swap(ny))
    y_pair = lax.ppermute(y_pair, "gy", pair_swap(ny))
    collided = pl.pallas_call(
        collide_kernel,
        out_shape=VMEM((27 * PLANES, COLS), F32),
        in_specs=[WHOLE],
        compiler_params=params(16),
        cost_estimate=pl.CostEstimate(flops=10**9, bytes_accessed=5 * 10**6, transcendentals=0),
        name="collide",
    )(arrived)
    x_pair, x_other = pl.pallas_call(
        edge_kernel,
        out_shape=(edge, edge),
        in_specs=[WHOLE] * 3,
        compiler_params=params(16),
        name="edges",
    )(collided, y_pair, y_other)
    x_other = lax.ppermute(x_other, "gx", other_swap(nx))
    x_pair = lax.ppermute(x_pair, "gx", pair_swap(nx))
    tables = [t.reshape(LINKS // COLS, COLS) for t in (link_cell, link_dir, link_q, link_panel)]
    tables = pl.pallas_call(
        table_kernel,
        out_shape=(
            VMEM((3 * PLANES, COLS), F32),
            VMEM((PLANES, LINKS), BF16),
            VMEM((COLS, LINKS), BF16),
            VMEM((PAN_DEV, LINKS), BF16),
            VMEM((24, LINKS), F32),
            VMEM((24, DEPTH * COLS), F32),
            VMEM((PAN_DEV, DEPTH * COLS), BF16),
        ),
        in_specs=[WHOLE] * 4,
        scratch_shapes=[VMEM((PLANES, 4 * COLS), F32)],
        compiler_params=params(16),
        cost_estimate=pl.CostEstimate(flops=6 * 10**9, bytes_accessed=70000, transcendentals=0),
        name="tables",
    )(*tables)
    *tables, late_push, late_pan = tables
    dense = tables[0]
    moved, bounce, force = pl.pallas_call(
        stream_kernel,
        out_shape=(
            VMEM((27 * PLANES, COLS), F32),
            VMEM((PLANES, COLS), F32),
            VMEM((24, PAN_DEV), F32),
        ),
        in_specs=[WHOLE] * 9,
        scratch_shapes=[
            VMEM((2, DEPTH, COLS), F32),
            VMEM((2, 9, DEPTH, COLS), F32),
            VMEM((PLANES, COLS), F32),
        ],
        compiler_params=params(24),
        name="stream",
    )(collided, y_pair, y_other, x_pair, *tables)
    own, to_pair, to_other = pl.pallas_call(
        late_kernel,
        out_shape=(small, small, small),
        in_specs=[WHOLE] * 5,
        compiler_params=params(16),
        name="late",
    )(x_other, dense, force, late_push, late_pan)
    from_other = lax.ppermute(to_other, "gx", other_swap(nx))
    from_pair = lax.ppermute(to_pair, "gx", pair_swap(nx))
    populations_next, _, _ = pl.pallas_call(
        finish_kernel,
        out_shape=(
            jax.ShapeDtypeStruct((27 * PLANES, COLS), F32),
            VMEM((27 * PLANES, COLS), F32),
            VMEM((PLANES, COLS), F32),
        ),
        in_specs=[WHOLE] * 5,
        out_specs=(SOMEWHERE, WHOLE, WHOLE),
        input_output_aliases={0: 1, 1: 2},
        scratch_shapes=[pltpu.SemaphoreType.DMA],
        compiler_params=params(16),
        name="finish",
    )(moved, bounce, x_other, dense, solid_mask.reshape(PLANES, COLS))
    return populations_next.reshape(populations.shape), (own + from_pair + from_other)[:3]


def solution(mesh):
    return jax.shard_map(
        per_device,
        mesh=mesh,
        in_specs=(
            P(None, None, "gx", "gy"),
            P(None, "gx", "gy"),
            P(("gx", "gy")),
            P(("gx", "gy")),
            P(("gx", "gy")),
            P(("gx", "gy")),
            P(("gx", "gy")),
        ),
        out_specs=(P(None, None, "gx", "gy"), P(None, ("gx", "gy"))),
        check_vma=False,
    )
```

```python
import functools

import jax
import jax.numpy as jnp
from jax import lax
from jax.experimental import pallas as pl
from jax.experimental.pallas import tpu as pltpu
from jax.sharding import PartitionSpec as P

PAN_DEV = 128
RELAXATION = 1.7
DEPTH, ROWS, COLS = 24, 8, 128
PLANES = DEPTH * ROWS
LINKS = 4096
HALF = DEPTH // 2
CHUNKS = 4
UNROLL_A = 3
UNROLL_T = 8
UNROLL_S = 11
UNROLL_G = 1
UNROLL_F = 6
OUT_COPIES = 4
TABLE_WIDTH = 512
GATHER_WIDTH = 4096
F32 = jnp.float32
BF16 = jnp.bfloat16
VMEM = pltpu.VMEM
WHOLE = pl.BlockSpec(memory_space=pltpu.VMEM)
SOMEWHERE = pl.BlockSpec(memory_space=pl.ANY)
HBM = pl.BlockSpec(memory_space=pltpu.HBM)


def params(mib):
    return pltpu.CompilerParams(vmem_limit_bytes=mib * 2**20)


def plane_rows(index, z):
    return pl.ds(pl.multiple_of((index * DEPTH + z) * ROWS, ROWS), ROWS)


def inverse_map(m0, m1, m2, u):
    if m0 is None and m1 is None and m2 is None:
        return None, None, None
    w = None if m0 is None else u * m0
    if m1 is not None:
        w = m1 if w is None else w + m1
    t = None
    if w is not None:
        t = u * (w if m1 is None else w + m1)
    if m2 is not None:
        t = m2 if t is None else t + m2
    if w is None:
        return t, -t, t
    return t - w, (-t if m0 is None else m0 - t), t + w


def collide(f):
    def at(a, b, c):
        return f[a * 9 + b * 3 + c]

    ends = [[at(a, b, 2) + at(a, b, 0) for b in range(3)] for a in range(3)]
    dz = [[at(a, b, 2) - at(a, b, 0) for b in range(3)] for a in range(3)]
    s = [[ends[a][b] + at(a, b, 1) for b in range(3)] for a in range(3)]
    row = [s[a][0] + s[a][1] + s[a][2] for a in range(3)]
    density = row[0] + row[1] + row[2]
    q0 = s[0][0] + s[1][0] + s[2][0]
    q2 = s[0][2] + s[1][2] + s[2][2]
    dzx = [dz[a][0] + dz[a][1] + dz[a][2] for a in range(3)]
    dzy0 = dz[0][0] + dz[1][0] + dz[2][0]
    dzy2 = dz[0][2] + dz[1][2] + dz[2][2]
    pzz = sum(ends[a][b] for a in range(3) for b in range(3))
    inv = 1.0 / density
    ux = (row[2] - row[0]) * inv
    uy = (q2 - q0) * inv
    uz = (dzx[0] + dzx[1] + dzx[2]) * inv
    keep = 1.0 - RELAXATION
    third = RELAXATION / 3.0

    def spread(p, first, second):
        return keep * (p * inv - first * second)

    xx = spread(row[2] + row[0], ux, ux) + third
    yy = spread(q2 + q0, uy, uy) + third
    zz = spread(pzz, uz, uz) + third
    xy = spread((s[2][2] - s[2][0]) + (s[0][0] - s[0][2]), ux, uy)
    xz = spread(dzx[2] - dzx[0], ux, uz)
    yz = spread(dzy2 - dzy0, uy, uz)
    xy2, xz2, yz2 = 2.0 * xy, 2.0 * xz, 2.0 * yz
    e220 = xx * yy + xy2 * xy
    e202 = xx * zz + xz2 * xz
    eyz = yy * zz + yz2 * yz
    e211 = xx * yz + xy2 * xz
    e121 = yy * xz + xy2 * yz
    e112 = zz * xy + xz2 * yz
    e222 = xx * eyz + xz2 * e121 + xy2 * e112
    k = {
        (0, 0, 0): jnp.ones_like(density),
        (2, 0, 0): xx,
        (0, 2, 0): yy,
        (0, 0, 2): zz,
        (1, 1, 0): xy,
        (1, 0, 1): xz,
        (0, 1, 1): yz,
        (2, 2, 0): e220,
        (2, 0, 2): e202,
        (0, 2, 2): eyz,
        (2, 1, 1): e211,
        (1, 2, 1): e121,
        (1, 1, 2): e112,
        (2, 2, 2): e222,
    }
    along_z, along_y, result = {}, {}, [None] * 27
    for a in range(3):
        for b in range(3):
            out = inverse_map(k.get((a, b, 0)), k.get((a, b, 1)), k.get((a, b, 2)), uz)
            for c in range(3):
                along_z[a, b, c] = out[c]
    for a in range(3):
        for c in range(3):
            out = inverse_map(along_z[a, 0, c], along_z[a, 1, c], along_z[a, 2, c], uy)
            for b in range(3):
                along_y[a, b, c] = out[b]
    scale = [density, 0.5 * density, 0.25 * density, 0.125 * density]
    for b in range(3):
        for c in range(3):
            out = inverse_map(along_y[0, b, c], along_y[1, b, c], along_y[2, b, c], ux)
            for a in range(3):
                moving = abs(a - 1) + abs(b - 1) + abs(c - 1)
                result[a * 9 + b * 3 + c] = scale[moving] * out[a]
    return result


def rim_kernel(pop_ref, buf_ref, near_ref, far_ref, stacked, turned, sem):
    even = lax.rem(lax.axis_index("gy"), 2) == 0
    step = DEPTH // CHUNKS
    copies = [
        pltpu.make_async_copy(
            pop_ref.at[:, pl.ds(i * step, step)], buf_ref.at[:, pl.ds(i * step, step)], sem.at[i]
        )
        for i in range(CHUNKS)
    ]
    for copy in copies:
        copy.start()
    stacked[...] = jnp.zeros_like(stacked)
    lane = lax.broadcasted_iota(jnp.int32, (ROWS, COLS), 1)
    packed = [None] * 27
    for z in range(DEPTH):
        if z % step == 0:
            copies[z // step].wait()
        here = lane // 2 == z
        for d in range(27):
            plane = pltpu.roll(buf_ref[d, z], 2 * z + 1, 1)
            packed[d] = plane if z == 0 else jnp.where(here, plane, packed[d])
    f = collide(packed)
    odd = lane % 2 == 1
    group = lane // 48
    for side in range(2):
        rim = []
        for v in range(3):
            value = jnp.zeros((ROWS, COLS), F32)
            for k in range(4 * v, min(4 * v + 4, 9)):
                d = k // 3 * 9 + k % 3 + (6 if side == 1 else 0)
                place = k % 4
                shift = (place // 2) * 48 + place % 2 - (0 if side == 1 else 1)
                moved = f[d] if shift == 0 else pltpu.roll(f[d], shift % COLS, 1)
                mine = (group == place // 2) & (odd == (place % 2 == 1))
                value = jnp.where(mine, moved, value)
            rim.append(value)
        for v in range(3):
            at = slice(v * ROWS, (v + 1) * ROWS)

            @pl.when(even == (side == 1))
            def _():
                near_ref[at, :] = rim[v]

            @pl.when(even != (side == 1))
            def _():
                far_ref[at, :] = rim[v]

        for end in range(2):
            for c in range(3):
                d = end * 18 + c + (6 if side == 1 else 0)
                x = end * (ROWS - 1)
                place = end * 3 + c + side * 8
                stacked[place : place + 1, :] = f[d][x : x + 1, :]
    turned[...] = stacked[...].T
    low = turned[pl.ds(1, DEPTH, stride=2), :]
    high = turned[pl.ds(0, DEPTH, stride=2), :]
    near_ref[DEPTH:, :] = jnp.where(even, high, low)
    far_ref[DEPTH:, :] = jnp.where(even, low, high)


def collide_kernel(buf_ref, col_ref):
    def body(z, carry):
        f = collide([buf_ref[d, z] for d in range(27)])
        for d in range(27):
            col_ref[plane_rows(d, z), :] = f[d]
        return carry

    lax.fori_loop(0, DEPTH, body, 0, unroll=UNROLL_A)


def edge_kernel(col_ref, near_ref, far_ref, pair_ref, other_ref):
    even = lax.rem(lax.axis_index("gy"), 2) == 0
    even_x = lax.rem(lax.axis_index("gx"), 2) == 0
    lane = lax.broadcasted_iota(jnp.int32, (DEPTH, COLS), 1)
    low = jnp.where(even, far_ref[DEPTH:, :], near_ref[DEPTH:, :])
    high = jnp.where(even, near_ref[DEPTH:, :], far_ref[DEPTH:, :])
    for end in range(2):
        rows = []
        for b in range(3):
            for c in range(3):
                start = (end * 18 + b * 3 + c) * PLANES + end * (ROWS - 1)
                row = col_ref[pl.ds(start, DEPTH, stride=ROWS), :]
                spot = end * 3 + c
                if b == 2:
                    halo = pltpu.roll(low, COLS - spot - 8, 1)
                    row = jnp.where(lane == 0, halo, pltpu.roll(row, 1, 1))
                elif b == 0:
                    halo = pltpu.roll(high, COLS - 1 - spot, 1)
                    row = jnp.where(lane == COLS - 1, halo, pltpu.roll(row, COLS - 1, 1))
                rows.append(row)

        @pl.when(even_x == (end == 1))
        def _():
            for k in range(9):
                pair_ref[k] = rows[k]

        @pl.when(even_x != (end == 1))
        def _():
            for k in range(9):
                other_ref[k] = rows[k]


def split_code(code):
    offset = jnp.where(code > 108.5, 2.0, jnp.where(code > 54.5, 1.0, 0.0))
    code = code - 54.0 * offset
    near = code > 27.5
    return offset, near, jnp.where(near, code - 28.0, code - 1.0)


def table_kernel(
    cell_ref, dir_ref, q_ref, panel_ref,
    dense_ref, row_ref, lane_ref, pan_ref, push_ref, late_push_ref, late_pan_ref,
    gathered,
):
    gx = lax.axis_index("gx")
    count = lax.axis_size("gx")
    per_row = PAN_DEV * lax.axis_size("gy")
    width = TABLE_WIDTH
    row_iota = lax.broadcasted_iota(jnp.int32, (PLANES, width), 0).astype(F32).astype(BF16)
    lane_iota = lax.broadcasted_iota(jnp.int32, (COLS, width), 0).astype(F32).astype(BF16)
    one, zero = jnp.ones((), BF16), jnp.zeros((), BF16)
    push_iota = lax.broadcasted_iota(jnp.int32, (24, width), 0)
    gathered[...] = jnp.zeros_like(gathered)

    def load(ref, i):
        n = width // COLS
        return jnp.concatenate([ref[pl.ds(n * i + j, 1), :] for j in range(n)], axis=1)

    def spread(value, count):
        tile = jnp.broadcast_to(value.astype(F32), (16, width)).astype(BF16)
        return jnp.concatenate([tile] * (count // 16), axis=0)

    def body(i, carry):
        at = pl.ds(pl.multiple_of(i * width, width), width)
        cell, direction = load(cell_ref, i), load(dir_ref, i)
        q, panel = load(q_ref, i), load(panel_ref, i)
        active = panel >= 0
        near = q < 0.5
        twice = 2.0 * q
        weight = jnp.where(near, twice, 1.0 / twice)
        weight_hi = weight.astype(BF16).astype(F32)
        weight_lo = weight - weight_hi
        offset = panel // per_row - gx + 1
        offset = jnp.where(offset < 0, offset + count, offset)
        offset = jnp.where(offset >= count, offset - count, offset)
        code = (direction + 1 + jnp.where(near, 27, 0) + 54 * offset).astype(F32)
        spot = panel % PAN_DEV
        row = jnp.where(active, cell // COLS, -1)
        rows = jnp.where(row_iota == spread(row, PLANES), one, zero)
        row_ref[:, at] = rows
        here = lane_iota == spread(cell % COLS, COLS)
        lane_ref[:, at] = jnp.where(here, one, zero)
        values = jnp.concatenate(
            [
                jnp.where(here, spread(v, COLS), zero)
                for v in (weight_hi, weight_lo, code, spot)
            ],
            axis=0,
        )
        gathered[...] += lax.dot_general(
            rows, values, (((1,), (1,)), ((), ())), preferred_element_type=F32
        )
        pan_ref[:, at] = jnp.where(lane_iota == spread(spot, PAN_DEV), one, zero)
        part = push_iota % 8
        step = jnp.where(
            part == 0,
            direction // 9 - 1,
            jnp.where(part == 1, direction // 3 % 3 - 1, direction % 3 - 1),
        )
        chosen = active & (push_iota // 8 == offset) & (part < 3)
        push_ref[:, at] = jnp.where(chosen, step, 0).astype(F32)
        return carry

    lax.fori_loop(0, LINKS // width, body, 0, unroll=UNROLL_T)
    dense_ref[:PLANES, :] = gathered[:, :COLS] + gathered[:, COLS : 2 * COLS]
    dense_ref[PLANES : 2 * PLANES, :] = gathered[:, 2 * COLS : 3 * COLS]
    dense_ref[2 * PLANES :, :] = gathered[:, 3 * COLS :]

    even_x = lax.rem(gx, 2) == 0
    last = jnp.where(even_x, 0, ROWS - 1)
    picked = [dense_ref[pl.ds(i * PLANES + last, DEPTH, stride=ROWS), :] for i in range(3)]
    offset, near, which = split_code(picked[1])
    lead = jnp.where(even_x, 18.0, 0.0)
    across = near & (which >= lead) & (which < lead + 9.0)
    share = jnp.where(across, 1.0 - picked[0], 0.0)
    k = jnp.where(across, which - lead, 0.0)
    step_y = jnp.where(k > 5.5, 1.0, jnp.where(k > 2.5, 0.0, -1.0))
    step_z = k - 3.0 * step_y - 4.0
    step_x = jnp.where(even_x, share, -share)
    step_y, step_z = step_y * share, step_z * share
    push_iota = lax.broadcasted_iota(jnp.int32, (24, COLS), 0)
    part, owner = push_iota % 8, (push_iota // 8).astype(F32)
    pan_iota = lax.broadcasted_iota(jnp.int32, (PAN_DEV, COLS), 0).astype(F32)
    for z in range(DEPTH):
        row = slice(z, z + 1)
        steps = jnp.where(
            part == 0,
            step_x[row],
            jnp.where(part == 1, step_y[row], jnp.where(part == 2, step_z[row], 0.0)),
        )
        at = slice(z * COLS, (z + 1) * COLS)
        late_push_ref[:, at] = jnp.where(owner == offset[row], steps, 0.0)
        late_pan_ref[:, at] = jnp.where(pan_iota == picked[2][row], 1.0, 0.0).astype(BF16)


def by_panel(push, pan):
    push_hi = push.astype(BF16).astype(F32)
    push = jnp.concatenate([push_hi, push - push_hi], axis=0).astype(BF16)
    return lax.dot_general(push, pan, (((1,), (1,)), ((), ())), preferred_element_type=F32)


def stream_kernel(
    col_ref, near_ref, far_ref, pair_ref, dense_ref, row_ref, lane_ref, pan_ref, push_ref,
    new_ref, bounce_ref, force_ref,
    edges, halo, momentum,
):
    even = lax.rem(lax.axis_index("gy"), 2) == 0
    even_x = lax.rem(lax.axis_index("gx"), 2) == 0
    halo[0] = jnp.where(even_x, 0.0, pair_ref[...])
    halo[1] = jnp.where(even_x, pair_ref[...], 0.0)
    edges[0] = jnp.where(even, far_ref[:DEPTH, :], near_ref[:DEPTH, :])
    edges[1] = jnp.where(even, near_ref[:DEPTH, :], far_ref[:DEPTH, :])
    sub = lax.broadcasted_iota(jnp.int32, (ROWS, COLS), 0)
    lane = lax.broadcasted_iota(jnp.int32, (ROWS, COLS), 1)

    def body(z, bottom, top):
        here_rows = pl.ds(pl.multiple_of(z * ROWS, ROWS), ROWS)
        code = dense_ref[pl.ds(pl.multiple_of(PLANES + z * ROWS, ROWS), ROWS), :]
        weight = dense_ref[here_rows, :]
        _, near, which = split_code(code)
        toward = jnp.zeros((ROWS, COLS), F32)
        second, reverse = toward, toward
        for d in range(27):
            a, b, c = d // 9, d // 3 % 3, d % 3
            here = col_ref[plane_rows(d, z), :]
            back = col_ref[plane_rows(26 - d, z), :]
            if (c == 2 and bottom) or (c == 0 and top):
                moved = back
            else:
                zs = z - (c - 1)
                moved = col_ref[plane_rows(d, zs), :]
                k = a * 3 + c
                spot = 2 * zs + k % 4 // 2 * 48 + k % 2
                at = slice(k // 4 * ROWS, k // 4 * ROWS + ROWS)
                if b == 2:
                    side = pltpu.roll(edges[0, at, :], COLS - spot, 1)
                    moved = jnp.where(lane == 0, side, pltpu.roll(moved, 1, 1))
                elif b == 0:
                    side = pltpu.roll(edges[1, at, :], COLS - 1 - spot, 1)
                    moved = jnp.where(lane == COLS - 1, side, pltpu.roll(moved, COLS - 1, 1))
                if a == 2:
                    edge = halo[0, b * 3 + c, pl.ds(zs, 1), :]
                    moved = jnp.where(sub == 0, edge, pltpu.roll(moved, 1, 0))
                elif a == 0:
                    edge = halo[1, b * 3 + c, pl.ds(zs, 1), :]
                    moved = jnp.where(sub == ROWS - 1, edge, pltpu.roll(moved, ROWS - 1, 0))
            new_ref[plane_rows(d, z), :] = moved
            if d != 13:
                match = which == float(d)
                toward = jnp.where(match, here, toward)
                second = jnp.where(match, moved, second)
                reverse = jnp.where(match, back, reverse)
        other = jnp.where(near, second, reverse)
        bounce = other + weight * (toward - other)
        momentum[here_rows, :] = jnp.where(code > 0.5, toward + bounce, 0.0)
        bounce_ref[here_rows, :] = bounce

    body(0, True, False)
    lax.fori_loop(
        1, DEPTH - 1, lambda z, carry: (body(z, False, False), carry)[1], 0, unroll=UNROLL_S
    )
    body(DEPTH - 1, False, True)

    turned = momentum[...].T
    turned_hi = turned.astype(BF16).astype(F32)
    turned = jnp.concatenate([turned_hi, turned - turned_hi], axis=0).astype(BF16)
    width = GATHER_WIDTH

    def gather(i, total):
        at = pl.ds(pl.multiple_of(i * width, width), width)
        rows = row_ref[:, at]
        picked = jnp.dot(turned, rows, preferred_element_type=F32)
        picked = picked[:COLS] + picked[COLS:]
        value = jnp.sum(picked * lane_ref[:, at].astype(F32), axis=0, keepdims=True)
        return total + by_panel(push_ref[:, at] * value, pan_ref[:, at])

    total = lax.fori_loop(
        0, LINKS // width, gather, jnp.zeros((48, PAN_DEV), F32), unroll=UNROLL_G
    )
    force_ref[...] = total[:24] + total[24:]


def late_row(dense_ref, even_x):
    last = jnp.where(even_x, 0, ROWS - 1)
    weight = dense_ref[pl.ds(last, DEPTH, stride=ROWS), :]
    _, near, which = split_code(dense_ref[pl.ds(PLANES + last, DEPTH, stride=ROWS), :])
    return near, which, weight


def late_kernel(other_ref, dense_ref, force_ref, late_push_ref, late_pan_ref, own_ref, send_pair_ref, send_other_ref):
    even_x = lax.rem(lax.axis_index("gx"), 2) == 0
    near, which, weight = late_row(dense_ref, even_x)
    lead = jnp.where(even_x, 18.0, 0.0)
    second = jnp.zeros((DEPTH, COLS), F32)
    for k in range(9):
        row = other_ref[k]
        if k % 3 == 2:
            row = pltpu.roll(row, 1, 0)
        elif k % 3 == 0:
            row = pltpu.roll(row, DEPTH - 1, 0)
        second = jnp.where(which == lead + float(k), row, second)
    second = jnp.concatenate([second[z : z + 1] for z in range(DEPTH)], axis=1)
    late = by_panel(late_push_ref[...] * second, late_pan_ref[...])
    force = force_ref[...] + late[:24] + late[24:]
    own_ref[...] = force[8:16]
    send_pair_ref[...] = jnp.where(even_x, force[16:24], force[0:8])
    send_other_ref[...] = jnp.where(even_x, force[0:8], force[16:24])


def finish_kernel(
    new_in_ref, bounce_in_ref, other_ref, dense_ref, mask_ref, out_ref, new_ref, bounce_ref, sem
):
    del new_in_ref, bounce_in_ref
    even_x = lax.rem(lax.axis_index("gx"), 2) == 0
    near, which, weight = late_row(dense_ref, even_x)
    last = jnp.where(even_x, 0, ROWS - 1)
    lead_index = jnp.where(even_x, 18, 0)
    lead = lead_index.astype(F32)
    level = lax.broadcasted_iota(jnp.int32, (DEPTH, COLS), 0)
    second = jnp.zeros((DEPTH, COLS), F32)
    for k in range(9):
        row = other_ref[k]
        at = pl.ds((lead_index + k) * PLANES + last, DEPTH, stride=ROWS)
        if k % 3 == 1:
            new_ref[at, :] = row
        else:
            row = pltpu.roll(row, 1 if k % 3 == 2 else DEPTH - 1, 0)
            inside = level > 0 if k % 3 == 2 else level < DEPTH - 1
            new_ref[at, :] = jnp.where(inside, row, new_ref[at, :])
        second = jnp.where(near & (which == lead + float(k)), row, second)
    at = pl.ds(last, DEPTH, stride=ROWS)
    bounce_ref[at, :] = bounce_ref[at, :] + (1.0 - weight) * second

    def body(z, carry):
        here_rows = pl.ds(pl.multiple_of(z * ROWS, ROWS), ROWS)
        _, _, target = split_code(dense_ref[pl.ds(pl.multiple_of(PLANES + z * ROWS, ROWS), ROWS), :])
        bounce = bounce_ref[here_rows, :]
        fluid = (1 - mask_ref[here_rows, :]).astype(F32)
        for d in range(27):
            value = new_ref[plane_rows(d, z), :]
            if d != 13:
                value = jnp.where(target == float(26 - d), bounce, value)
            new_ref[plane_rows(d, z), :] = value * fluid
        return carry

    copies = []
    for i in range(OUT_COPIES):
        depth = DEPTH // OUT_COPIES
        lax.fori_loop(i * depth, (i + 1) * depth, body, 0, unroll=UNROLL_F)
        at = pl.ds(i * depth * ROWS, depth * ROWS)
        copies.append(
            pltpu.make_async_copy(
                new_ref.reshape(27, PLANES, COLS).at[:, at], out_ref.at[:, at], sem.at[i]
            )
        )
        copies[i].start()
    for copy in copies:
        copy.wait()


def pair_swap(count):
    return [(i, i ^ 1) for i in range(count)]


def other_swap(count):
    return [(i, (i + 1) % count if i % 2 else (i - 1) % count) for i in range(count)]


def per_device(populations, solid_mask, link_cell, link_dir, link_second, link_q, link_panel):
    nx, ny = lax.axis_size("gx"), lax.axis_size("gy")
    small = jax.ShapeDtypeStruct((ROWS, PAN_DEV), F32)
    column = jax.ShapeDtypeStruct((2 * DEPTH, COLS), F32)
    edge = jax.ShapeDtypeStruct((9, DEPTH, COLS), F32)
    arrived, y_pair, y_other = pl.pallas_call(
        rim_kernel,
        out_shape=(VMEM(populations.shape, F32), column, column),
        in_specs=[HBM],
        scratch_shapes=[
            VMEM((COLS, COLS), F32),
            VMEM((COLS, COLS), F32),
            pltpu.SemaphoreType.DMA((CHUNKS,)),
        ],
        compiler_params=params(16),
        name="rims",
    )(pltpu.with_memory_space_constraint(populations, pltpu.HBM))
    y_other = lax.ppermute(y_other, "gy", other_swap(ny))
    y_pair = lax.ppermute(y_pair, "gy", pair_swap(ny))
    collided = pl.pallas_call(
        collide_kernel,
        out_shape=VMEM((27 * PLANES, COLS), F32),
        in_specs=[WHOLE],
        compiler_params=params(16),
        cost_estimate=pl.CostEstimate(flops=10**9, bytes_accessed=5 * 10**6, transcendentals=0),
        name="collide",
    )(arrived)
    x_pair, x_other = pl.pallas_call(
        edge_kernel,
        out_shape=(edge, edge),
        in_specs=[WHOLE] * 3,
        compiler_params=params(16),
        name="edges",
    )(collided, y_pair, y_other)
    x_other = lax.ppermute(x_other, "gx", other_swap(nx))
    x_pair = lax.ppermute(x_pair, "gx", pair_swap(nx))
    tables = [t.reshape(LINKS // COLS, COLS) for t in (link_cell, link_dir, link_q, link_panel)]
    tables = pl.pallas_call(
        table_kernel,
        out_shape=(
            VMEM((3 * PLANES, COLS), F32),
            VMEM((PLANES, LINKS), BF16),
            VMEM((COLS, LINKS), BF16),
            VMEM((PAN_DEV, LINKS), BF16),
            VMEM((24, LINKS), F32),
            VMEM((24, DEPTH * COLS), F32),
            VMEM((PAN_DEV, DEPTH * COLS), BF16),
        ),
        in_specs=[WHOLE] * 4,
        scratch_shapes=[VMEM((PLANES, 4 * COLS), F32)],
        compiler_params=params(16),
        cost_estimate=pl.CostEstimate(flops=6 * 10**9, bytes_accessed=70000, transcendentals=0),
        name="tables",
    )(*tables)
    *tables, late_push, late_pan = tables
    dense = tables[0]
    moved, bounce, force = pl.pallas_call(
        stream_kernel,
        out_shape=(
            VMEM((27 * PLANES, COLS), F32),
            VMEM((PLANES, COLS), F32),
            VMEM((24, PAN_DEV), F32),
        ),
        in_specs=[WHOLE] * 9,
        scratch_shapes=[
            VMEM((2, DEPTH, COLS), F32),
            VMEM((2, 9, DEPTH, COLS), F32),
            VMEM((PLANES, COLS), F32),
        ],
        compiler_params=params(24),
        name="stream",
    )(collided, y_pair, y_other, x_pair, *tables)
    own, to_pair, to_other = pl.pallas_call(
        late_kernel,
        out_shape=(small, small, small),
        in_specs=[WHOLE] * 5,
        compiler_params=params(16),
        name="late",
    )(x_other, dense, force, late_push, late_pan)
    from_other = lax.ppermute(to_other, "gx", other_swap(nx))
    from_pair = lax.ppermute(to_pair, "gx", pair_swap(nx))
    populations_next, _, _ = pl.pallas_call(
        finish_kernel,
        out_shape=(
            jax.ShapeDtypeStruct((27, PLANES, COLS), F32),
            VMEM((27 * PLANES, COLS), F32),
            VMEM((PLANES, COLS), F32),
        ),
        in_specs=[WHOLE] * 5,
        out_specs=(SOMEWHERE, WHOLE, WHOLE),
        input_output_aliases={0: 1, 1: 2},
        scratch_shapes=[pltpu.SemaphoreType.DMA((OUT_COPIES,))],
        compiler_params=params(16),
        name="finish",
    )(moved, bounce, x_other, dense, solid_mask.reshape(PLANES, COLS))
    return populations_next.reshape(populations.shape), (own + from_pair + from_other)[:3]


def solution(mesh):
    return jax.shard_map(
        per_device,
        mesh=mesh,
        in_specs=(
            P(None, None, "gx", "gy"),
            P(None, "gx", "gy"),
            P(("gx", "gy")),
            P(("gx", "gy")),
            P(("gx", "gy")),
            P(("gx", "gy")),
            P(("gx", "gy")),
        ),
        out_specs=(P(None, None, "gx", "gy"), P(None, ("gx", "gy"))),
        check_vma=False,
    )
```

```python
import functools

import jax
import jax.numpy as jnp
from jax import lax
from jax.experimental import pallas as pl
from jax.experimental.pallas import tpu as pltpu
from jax.sharding import PartitionSpec as P

PAN_DEV = 128
RELAXATION = 1.7
DEPTH, ROWS, COLS = 24, 8, 128
PLANES = DEPTH * ROWS
LINKS = 4096
HALF = DEPTH // 2
CHUNKS = 4
UNROLL_A = 3
UNROLL_T = 8
UNROLL_S = 11
UNROLL_G = 1
UNROLL_F = 6
OUT_COPIES = 4
TABLE_WIDTH = 512
GATHER_WIDTH = 4096
F32 = jnp.float32
BF16 = jnp.bfloat16
VMEM = pltpu.VMEM
WHOLE = pl.BlockSpec(memory_space=pltpu.VMEM)
SOMEWHERE = pl.BlockSpec(memory_space=pl.ANY)
HBM = pl.BlockSpec(memory_space=pltpu.HBM)


def params(mib):
    return pltpu.CompilerParams(vmem_limit_bytes=mib * 2**20)


def plane_rows(index, z):
    return pl.ds(pl.multiple_of((index * DEPTH + z) * ROWS, ROWS), ROWS)


def inverse_map(m0, m1, m2, u):
    if m0 is None and m1 is None and m2 is None:
        return None, None, None
    w = None if m0 is None else u * m0
    if m1 is not None:
        w = m1 if w is None else w + m1
    t = None
    if w is not None:
        t = u * (w if m1 is None else w + m1)
    if m2 is not None:
        t = m2 if t is None else t + m2
    if w is None:
        return t, -t, t
    return t - w, (-t if m0 is None else m0 - t), t + w


def collide(f):
    def at(a, b, c):
        return f[a * 9 + b * 3 + c]

    ends = [[at(a, b, 2) + at(a, b, 0) for b in range(3)] for a in range(3)]
    dz = [[at(a, b, 2) - at(a, b, 0) for b in range(3)] for a in range(3)]
    s = [[ends[a][b] + at(a, b, 1) for b in range(3)] for a in range(3)]
    row = [s[a][0] + s[a][1] + s[a][2] for a in range(3)]
    density = row[0] + row[1] + row[2]
    q0 = s[0][0] + s[1][0] + s[2][0]
    q2 = s[0][2] + s[1][2] + s[2][2]
    dzx = [dz[a][0] + dz[a][1] + dz[a][2] for a in range(3)]
    dzy0 = dz[0][0] + dz[1][0] + dz[2][0]
    dzy2 = dz[0][2] + dz[1][2] + dz[2][2]
    pzz = sum(ends[a][b] for a in range(3) for b in range(3))
    inv = 1.0 / density
    ux = (row[2] - row[0]) * inv
    uy = (q2 - q0) * inv
    uz = (dzx[0] + dzx[1] + dzx[2]) * inv
    keep = 1.0 - RELAXATION
    third = RELAXATION / 3.0

    def spread(p, first, second):
        return keep * (p * inv - first * second)

    xx = spread(row[2] + row[0], ux, ux) + third
    yy = spread(q2 + q0, uy, uy) + third
    zz = spread(pzz, uz, uz) + third
    xy = spread((s[2][2] - s[2][0]) + (s[0][0] - s[0][2]), ux, uy)
    xz = spread(dzx[2] - dzx[0], ux, uz)
    yz = spread(dzy2 - dzy0, uy, uz)
    xy2, xz2, yz2 = 2.0 * xy, 2.0 * xz, 2.0 * yz
    e220 = xx * yy + xy2 * xy
    e202 = xx * zz + xz2 * xz
    eyz = yy * zz + yz2 * yz
    e211 = xx * yz + xy2 * xz
    e121 = yy * xz + xy2 * yz
    e112 = zz * xy + xz2 * yz
    e222 = xx * eyz + xz2 * e121 + xy2 * e112
    k = {
        (0, 0, 0): jnp.ones_like(density),
        (2, 0, 0): xx,
        (0, 2, 0): yy,
        (0, 0, 2): zz,
        (1, 1, 0): xy,
        (1, 0, 1): xz,
        (0, 1, 1): yz,
        (2, 2, 0): e220,
        (2, 0, 2): e202,
        (0, 2, 2): eyz,
        (2, 1, 1): e211,
        (1, 2, 1): e121,
        (1, 1, 2): e112,
        (2, 2, 2): e222,
    }
    along_z, along_y, result = {}, {}, [None] * 27
    for a in range(3):
        for b in range(3):
            out = inverse_map(k.get((a, b, 0)), k.get((a, b, 1)), k.get((a, b, 2)), uz)
            for c in range(3):
                along_z[a, b, c] = out[c]
    for a in range(3):
        for c in range(3):
            out = inverse_map(along_z[a, 0, c], along_z[a, 1, c], along_z[a, 2, c], uy)
            for b in range(3):
                along_y[a, b, c] = out[b]
    scale = [density, 0.5 * density, 0.25 * density, 0.125 * density]
    for b in range(3):
        for c in range(3):
            out = inverse_map(along_y[0, b, c], along_y[1, b, c], along_y[2, b, c], ux)
            for a in range(3):
                moving = abs(a - 1) + abs(b - 1) + abs(c - 1)
                result[a * 9 + b * 3 + c] = scale[moving] * out[a]
    return result


def rim_kernel(pop_ref, buf_ref, near_ref, far_ref, stacked, turned, sem):
    even = lax.rem(lax.axis_index("gy"), 2) == 0
    step = DEPTH // CHUNKS
    copies = [
        pltpu.make_async_copy(
            pop_ref.at[:, pl.ds(i * step, step)], buf_ref.at[:, pl.ds(i * step, step)], sem.at[i]
        )
        for i in range(CHUNKS)
    ]
    for copy in copies:
        copy.start()
    stacked[...] = jnp.zeros_like(stacked)
    lane = lax.broadcasted_iota(jnp.int32, (ROWS, COLS), 1)
    packed = [None] * 27
    for z in range(DEPTH):
        if z % step == 0:
            copies[z // step].wait()
        here = lane // 2 == z
        for d in range(27):
            plane = pltpu.roll(buf_ref[d, z], 2 * z + 1, 1)
            packed[d] = plane if z == 0 else jnp.where(here, plane, packed[d])
    f = collide(packed)
    odd = lane % 2 == 1
    group = lane // 48
    for side in range(2):
        rim = []
        for v in range(3):
            value = jnp.zeros((ROWS, COLS), F32)
            for k in range(4 * v, min(4 * v + 4, 9)):
                d = k // 3 * 9 + k % 3 + (6 if side == 1 else 0)
                place = k % 4
                shift = (place // 2) * 48 + place % 2 - (0 if side == 1 else 1)
                moved = f[d] if shift == 0 else pltpu.roll(f[d], shift % COLS, 1)
                mine = (group == place // 2) & (odd == (place % 2 == 1))
                value = jnp.where(mine, moved, value)
            rim.append(value)
        for v in range(3):
            at = slice(v * ROWS, (v + 1) * ROWS)

            @pl.when(even == (side == 1))
            def _():
                near_ref[at, :] = rim[v]

            @pl.when(even != (side == 1))
            def _():
                far_ref[at, :] = rim[v]

        for end in range(2):
            for c in range(3):
                d = end * 18 + c + (6 if side == 1 else 0)
                x = end * (ROWS - 1)
                place = end * 3 + c + side * 8
                stacked[place : place + 1, :] = f[d][x : x + 1, :]
    turned[...] = stacked[...].T
    low = turned[pl.ds(1, DEPTH, stride=2), :]
    high = turned[pl.ds(0, DEPTH, stride=2), :]
    near_ref[DEPTH:, :] = jnp.where(even, high, low)
    far_ref[DEPTH:, :] = jnp.where(even, low, high)


def collide_kernel(buf_ref, col_ref):
    def body(z, carry):
        f = collide([buf_ref[d, z] for d in range(27)])
        for d in range(27):
            col_ref[plane_rows(d, z), :] = f[d]
        return carry

    lax.fori_loop(0, DEPTH, body, 0, unroll=UNROLL_A)


def edge_kernel(col_ref, near_ref, far_ref, pair_ref, other_ref):
    even = lax.rem(lax.axis_index("gy"), 2) == 0
    even_x = lax.rem(lax.axis_index("gx"), 2) == 0
    lane = lax.broadcasted_iota(jnp.int32, (DEPTH, COLS), 1)
    low = jnp.where(even, far_ref[DEPTH:, :], near_ref[DEPTH:, :])
    high = jnp.where(even, near_ref[DEPTH:, :], far_ref[DEPTH:, :])
    for end in range(2):
        rows = []
        for b in range(3):
            for c in range(3):
                start = (end * 18 + b * 3 + c) * PLANES + end * (ROWS - 1)
                row = col_ref[pl.ds(start, DEPTH, stride=ROWS), :]
                spot = end * 3 + c
                if b == 2:
                    halo = pltpu.roll(low, COLS - spot - 8, 1)
                    row = jnp.where(lane == 0, halo, pltpu.roll(row, 1, 1))
                elif b == 0:
                    halo = pltpu.roll(high, COLS - 1 - spot, 1)
                    row = jnp.where(lane == COLS - 1, halo, pltpu.roll(row, COLS - 1, 1))
                rows.append(row)

        @pl.when(even_x == (end == 1))
        def _():
            for k in range(9):
                pair_ref[k] = rows[k]

        @pl.when(even_x != (end == 1))
        def _():
            for k in range(9):
                other_ref[k] = rows[k]


def split_code(code):
    offset = jnp.where(code > 108.5, 2.0, jnp.where(code > 54.5, 1.0, 0.0))
    code = code - 54.0 * offset
    near = code > 27.5
    return offset, near, jnp.where(near, code - 28.0, code - 1.0)


def table_kernel(
    cell_ref, dir_ref, q_ref, panel_ref,
    dense_ref, row_ref, lane_ref, pan_ref, push_ref, late_push_ref, late_pan_ref,
    gathered, fields,
):
    gx = lax.axis_index("gx")
    count = lax.axis_size("gx")
    per_row = PAN_DEV * lax.axis_size("gy")
    width = TABLE_WIDTH
    row_iota = lax.broadcasted_iota(jnp.int32, (PLANES, width), 0).astype(F32).astype(BF16)
    lane_iota = lax.broadcasted_iota(jnp.int32, (COLS, width), 0).astype(F32).astype(BF16)
    one, zero = jnp.ones((), BF16), jnp.zeros((), BF16)
    push_iota = lax.broadcasted_iota(jnp.int32, (24, width), 0)
    part, owner = push_iota % 8, (push_iota // 8).astype(F32)
    gathered[...] = jnp.zeros_like(gathered)

    cell, direction, q, panel = cell_ref[...], dir_ref[...], q_ref[...], panel_ref[...]
    active = panel >= 0
    near = q < 0.5
    twice = 2.0 * q
    weight = jnp.where(near, twice, 1.0 / twice)
    weight_hi = weight.astype(BF16).astype(F32)
    offset = panel // per_row - gx + 1
    offset = jnp.where(offset < 0, offset + count, offset)
    offset = jnp.where(offset >= count, offset - count, offset)
    ninth, third = (direction * 57) >> 9, (direction * 43) >> 7
    numbers = (
        jnp.where(active, cell >> 7, -1),
        cell & 127,
        weight_hi,
        weight - weight_hi,
        direction + 1 + jnp.where(near, 27, 0) + 54 * offset,
        panel & 127,
        jnp.where(active, offset, -1),
        ninth - 1,
        third - 3 * ninth - 1,
        direction - 3 * third - 1,
    )
    for n, value in enumerate(numbers):
        fields[n] = value.astype(F32)

    def load(n, i):
        share = width // COLS
        return jnp.concatenate([fields[n, pl.ds(share * i + j, 1), :] for j in range(share)], axis=1)

    def spread(value, count):
        tile = jnp.broadcast_to(value.astype(F32), (16, width)).astype(BF16)
        return jnp.concatenate([tile] * (count // 16), axis=0)

    def body(i, carry):
        at = pl.ds(pl.multiple_of(i * width, width), width)
        rows = jnp.where(row_iota == spread(load(0, i), PLANES), one, zero)
        row_ref[:, at] = rows
        here = lane_iota == spread(load(1, i), COLS)
        lane_ref[:, at] = jnp.where(here, one, zero)
        spot = spread(load(5, i), COLS)
        values = [spread(load(n, i), COLS) for n in (2, 3, 4)] + [spot]
        gathered[...] += lax.dot_general(
            rows,
            jnp.concatenate([jnp.where(here, v, zero) for v in values], axis=0),
            (((1,), (1,)), ((), ())),
            preferred_element_type=F32,
        )
        pan_ref[:, at] = jnp.where(lane_iota == spot, one, zero)
        step = jnp.where(part == 0, load(7, i), jnp.where(part == 1, load(8, i), load(9, i)))
        push_ref[:, at] = jnp.where((owner == load(6, i)) & (part < 3), step, 0.0)
        return carry

    lax.fori_loop(0, LINKS // width, body, 0, unroll=UNROLL_T)
    dense_ref[:PLANES, :] = gathered[:, :COLS] + gathered[:, COLS : 2 * COLS]
    dense_ref[PLANES : 2 * PLANES, :] = gathered[:, 2 * COLS : 3 * COLS]
    dense_ref[2 * PLANES :, :] = gathered[:, 3 * COLS :]

    even_x = lax.rem(gx, 2) == 0
    last = jnp.where(even_x, 0, ROWS - 1)
    picked = [dense_ref[pl.ds(i * PLANES + last, DEPTH, stride=ROWS), :] for i in range(3)]
    offset, near, which = split_code(picked[1])
    lead = jnp.where(even_x, 18.0, 0.0)
    across = near & (which >= lead) & (which < lead + 9.0)
    share = jnp.where(across, 1.0 - picked[0], 0.0)
    k = jnp.where(across, which - lead, 0.0)
    step_y = jnp.where(k > 5.5, 1.0, jnp.where(k > 2.5, 0.0, -1.0))
    step_z = k - 3.0 * step_y - 4.0
    step_x = jnp.where(even_x, share, -share)
    step_y, step_z = step_y * share, step_z * share
    push_iota = lax.broadcasted_iota(jnp.int32, (24, COLS), 0)
    part, owner = push_iota % 8, (push_iota // 8).astype(F32)
    pan_iota = lax.broadcasted_iota(jnp.int32, (PAN_DEV, COLS), 0).astype(F32)
    for z in range(DEPTH):
        row = slice(z, z + 1)
        steps = jnp.where(
            part == 0,
            step_x[row],
            jnp.where(part == 1, step_y[row], jnp.where(part == 2, step_z[row], 0.0)),
        )
        at = slice(z * COLS, (z + 1) * COLS)
        late_push_ref[:, at] = jnp.where(owner == offset[row], steps, 0.0)
        late_pan_ref[:, at] = jnp.where(pan_iota == picked[2][row], 1.0, 0.0).astype(BF16)


def by_panel(push, pan):
    push_hi = push.astype(BF16).astype(F32)
    push = jnp.concatenate([push_hi, push - push_hi], axis=0).astype(BF16)
    return lax.dot_general(push, pan, (((1,), (1,)), ((), ())), preferred_element_type=F32)


def stream_kernel(
    col_ref, near_ref, far_ref, pair_ref, dense_ref, row_ref, lane_ref, pan_ref, push_ref,
    new_ref, bounce_ref, force_ref,
    edges, halo, momentum,
):
    even = lax.rem(lax.axis_index("gy"), 2) == 0
    even_x = lax.rem(lax.axis_index("gx"), 2) == 0
    halo[0] = jnp.where(even_x, 0.0, pair_ref[...])
    halo[1] = jnp.where(even_x, pair_ref[...], 0.0)
    edges[0] = jnp.where(even, far_ref[:DEPTH, :], near_ref[:DEPTH, :])
    edges[1] = jnp.where(even, near_ref[:DEPTH, :], far_ref[:DEPTH, :])
    sub = lax.broadcasted_iota(jnp.int32, (ROWS, COLS), 0)
    lane = lax.broadcasted_iota(jnp.int32, (ROWS, COLS), 1)

    def body(z, bottom, top):
        here_rows = pl.ds(pl.multiple_of(z * ROWS, ROWS), ROWS)
        code = dense_ref[pl.ds(pl.multiple_of(PLANES + z * ROWS, ROWS), ROWS), :]
        weight = dense_ref[here_rows, :]
        _, near, which = split_code(code)
        toward = jnp.zeros((ROWS, COLS), F32)
        second, reverse = toward, toward
        for d in range(27):
            a, b, c = d // 9, d // 3 % 3, d % 3
            here = col_ref[plane_rows(d, z), :]
            back = col_ref[plane_rows(26 - d, z), :]
            if (c == 2 and bottom) or (c == 0 and top):
                moved = back
            else:
                zs = z - (c - 1)
                moved = col_ref[plane_rows(d, zs), :]
                k = a * 3 + c
                spot = 2 * zs + k % 4 // 2 * 48 + k % 2
                at = slice(k // 4 * ROWS, k // 4 * ROWS + ROWS)
                if b == 2:
                    side = pltpu.roll(edges[0, at, :], COLS - spot, 1)
                    moved = jnp.where(lane == 0, side, pltpu.roll(moved, 1, 1))
                elif b == 0:
                    side = pltpu.roll(edges[1, at, :], COLS - 1 - spot, 1)
                    moved = jnp.where(lane == COLS - 1, side, pltpu.roll(moved, COLS - 1, 1))
                if a == 2:
                    edge = halo[0, b * 3 + c, pl.ds(zs, 1), :]
                    moved = jnp.where(sub == 0, edge, pltpu.roll(moved, 1, 0))
                elif a == 0:
                    edge = halo[1, b * 3 + c, pl.ds(zs, 1), :]
                    moved = jnp.where(sub == ROWS - 1, edge, pltpu.roll(moved, ROWS - 1, 0))
            new_ref[plane_rows(d, z), :] = moved
            if d != 13:
                match = which == float(d)
                toward = jnp.where(match, here, toward)
                second = jnp.where(match, moved, second)
                reverse = jnp.where(match, back, reverse)
        other = jnp.where(near, second, reverse)
        bounce = other + weight * (toward - other)
        momentum[here_rows, :] = jnp.where(code > 0.5, toward + bounce, 0.0)
        bounce_ref[here_rows, :] = bounce

    body(0, True, False)
    lax.fori_loop(
        1, DEPTH - 1, lambda z, carry: (body(z, False, False), carry)[1], 0, unroll=UNROLL_S
    )
    body(DEPTH - 1, False, True)

    turned = momentum[...].T
    turned_hi = turned.astype(BF16).astype(F32)
    turned = jnp.concatenate([turned_hi, turned - turned_hi], axis=0).astype(BF16)
    width = GATHER_WIDTH

    def gather(i, total):
        at = pl.ds(pl.multiple_of(i * width, width), width)
        rows = row_ref[:, at]
        picked = jnp.dot(turned, rows, preferred_element_type=F32)
        picked = picked[:COLS] + picked[COLS:]
        value = jnp.sum(picked * lane_ref[:, at].astype(F32), axis=0, keepdims=True)
        return total + by_panel(push_ref[:, at] * value, pan_ref[:, at])

    total = lax.fori_loop(
        0, LINKS // width, gather, jnp.zeros((48, PAN_DEV), F32), unroll=UNROLL_G
    )
    force_ref[...] = total[:24] + total[24:]


def late_row(dense_ref, even_x):
    last = jnp.where(even_x, 0, ROWS - 1)
    weight = dense_ref[pl.ds(last, DEPTH, stride=ROWS), :]
    _, near, which = split_code(dense_ref[pl.ds(PLANES + last, DEPTH, stride=ROWS), :])
    return near, which, weight


def late_kernel(other_ref, dense_ref, force_ref, late_push_ref, late_pan_ref, own_ref, send_pair_ref, send_other_ref):
    even_x = lax.rem(lax.axis_index("gx"), 2) == 0
    near, which, weight = late_row(dense_ref, even_x)
    lead = jnp.where(even_x, 18.0, 0.0)
    second = jnp.zeros((DEPTH, COLS), F32)
    for k in range(9):
        row = other_ref[k]
        if k % 3 == 2:
            row = pltpu.roll(row, 1, 0)
        elif k % 3 == 0:
            row = pltpu.roll(row, DEPTH - 1, 0)
        second = jnp.where(which == lead + float(k), row, second)
    second = jnp.concatenate([second[z : z + 1] for z in range(DEPTH)], axis=1)
    late = by_panel(late_push_ref[...] * second, late_pan_ref[...])
    force = force_ref[...] + late[:24] + late[24:]
    own_ref[...] = force[8:16]
    send_pair_ref[...] = jnp.where(even_x, force[16:24], force[0:8])
    send_other_ref[...] = jnp.where(even_x, force[0:8], force[16:24])


def finish_kernel(
    new_in_ref, bounce_in_ref, other_ref, dense_ref, mask_ref, out_ref, new_ref, bounce_ref, sem
):
    del new_in_ref, bounce_in_ref
    even_x = lax.rem(lax.axis_index("gx"), 2) == 0
    near, which, weight = late_row(dense_ref, even_x)
    last = jnp.where(even_x, 0, ROWS - 1)
    lead_index = jnp.where(even_x, 18, 0)
    lead = lead_index.astype(F32)
    level = lax.broadcasted_iota(jnp.int32, (DEPTH, COLS), 0)
    second = jnp.zeros((DEPTH, COLS), F32)
    for k in range(9):
        row = other_ref[k]
        at = pl.ds((lead_index + k) * PLANES + last, DEPTH, stride=ROWS)
        if k % 3 == 1:
            new_ref[at, :] = row
        else:
            row = pltpu.roll(row, 1 if k % 3 == 2 else DEPTH - 1, 0)
            inside = level > 0 if k % 3 == 2 else level < DEPTH - 1
            new_ref[at, :] = jnp.where(inside, row, new_ref[at, :])
        second = jnp.where(near & (which == lead + float(k)), row, second)
    at = pl.ds(last, DEPTH, stride=ROWS)
    bounce_ref[at, :] = bounce_ref[at, :] + (1.0 - weight) * second

    def body(z, carry):
        here_rows = pl.ds(pl.multiple_of(z * ROWS, ROWS), ROWS)
        _, _, target = split_code(dense_ref[pl.ds(pl.multiple_of(PLANES + z * ROWS, ROWS), ROWS), :])
        bounce = bounce_ref[here_rows, :]
        fluid = (1 - mask_ref[here_rows, :]).astype(F32)
        for d in range(27):
            value = new_ref[plane_rows(d, z), :]
            if d != 13:
                value = jnp.where(target == float(26 - d), bounce, value)
            new_ref[plane_rows(d, z), :] = value * fluid
        return carry

    copies = []
    for i in range(OUT_COPIES):
        depth = DEPTH // OUT_COPIES
        lax.fori_loop(i * depth, (i + 1) * depth, body, 0, unroll=UNROLL_F)
        at = pl.ds(i * depth * ROWS, depth * ROWS)
        copies.append(
            pltpu.make_async_copy(
                new_ref.reshape(27, PLANES, COLS).at[:, at], out_ref.at[:, at], sem.at[i]
            )
        )
        copies[i].start()
    for copy in copies:
        copy.wait()


def pair_swap(count):
    return [(i, i ^ 1) for i in range(count)]


def other_swap(count):
    return [(i, (i + 1) % count if i % 2 else (i - 1) % count) for i in range(count)]


def per_device(populations, solid_mask, link_cell, link_dir, link_second, link_q, link_panel):
    nx, ny = lax.axis_size("gx"), lax.axis_size("gy")
    small = jax.ShapeDtypeStruct((ROWS, PAN_DEV), F32)
    column = jax.ShapeDtypeStruct((2 * DEPTH, COLS), F32)
    edge = jax.ShapeDtypeStruct((9, DEPTH, COLS), F32)
    arrived, y_pair, y_other = pl.pallas_call(
        rim_kernel,
        out_shape=(VMEM(populations.shape, F32), column, column),
        in_specs=[HBM],
        scratch_shapes=[
            VMEM((COLS, COLS), F32),
            VMEM((COLS, COLS), F32),
            pltpu.SemaphoreType.DMA((CHUNKS,)),
        ],
        compiler_params=params(16),
        name="rims",
    )(pltpu.with_memory_space_constraint(populations, pltpu.HBM))
    y_other = lax.ppermute(y_other, "gy", other_swap(ny))
    y_pair = lax.ppermute(y_pair, "gy", pair_swap(ny))
    collided = pl.pallas_call(
        collide_kernel,
        out_shape=VMEM((27 * PLANES, COLS), F32),
        in_specs=[WHOLE],
        compiler_params=params(16),
        cost_estimate=pl.CostEstimate(flops=10**9, bytes_accessed=5 * 10**6, transcendentals=0),
        name="collide",
    )(arrived)
    x_pair, x_other = pl.pallas_call(
        edge_kernel,
        out_shape=(edge, edge),
        in_specs=[WHOLE] * 3,
        compiler_params=params(16),
        name="edges",
    )(collided, y_pair, y_other)
    x_other = lax.ppermute(x_other, "gx", other_swap(nx))
    x_pair = lax.ppermute(x_pair, "gx", pair_swap(nx))
    tables = [t.reshape(LINKS // COLS, COLS) for t in (link_cell, link_dir, link_q, link_panel)]
    tables = pl.pallas_call(
        table_kernel,
        out_shape=(
            VMEM((3 * PLANES, COLS), F32),
            VMEM((PLANES, LINKS), BF16),
            VMEM((COLS, LINKS), BF16),
            VMEM((PAN_DEV, LINKS), BF16),
            VMEM((24, LINKS), F32),
            VMEM((24, DEPTH * COLS), F32),
            VMEM((PAN_DEV, DEPTH * COLS), BF16),
        ),
        in_specs=[WHOLE] * 4,
        scratch_shapes=[
            VMEM((PLANES, 4 * COLS), F32),
            VMEM((10, LINKS // COLS, COLS), F32),
        ],
        compiler_params=params(16),
        cost_estimate=pl.CostEstimate(flops=6 * 10**9, bytes_accessed=70000, transcendentals=0),
        name="tables",
    )(*tables)
    *tables, late_push, late_pan = tables
    dense = tables[0]
    moved, bounce, force = pl.pallas_call(
        stream_kernel,
        out_shape=(
            VMEM((27 * PLANES, COLS), F32),
            VMEM((PLANES, COLS), F32),
            VMEM((24, PAN_DEV), F32),
        ),
        in_specs=[WHOLE] * 9,
        scratch_shapes=[
            VMEM((2, DEPTH, COLS), F32),
            VMEM((2, 9, DEPTH, COLS), F32),
            VMEM((PLANES, COLS), F32),
        ],
        compiler_params=params(24),
        name="stream",
    )(collided, y_pair, y_other, x_pair, *tables)
    own, to_pair, to_other = pl.pallas_call(
        late_kernel,
        out_shape=(small, small, small),
        in_specs=[WHOLE] * 5,
        compiler_params=params(16),
        name="late",
    )(x_other, dense, force, late_push, late_pan)
    from_other = lax.ppermute(to_other, "gx", other_swap(nx))
    from_pair = lax.ppermute(to_pair, "gx", pair_swap(nx))
    populations_next, _, _ = pl.pallas_call(
        finish_kernel,
        out_shape=(
            jax.ShapeDtypeStruct((27, PLANES, COLS), F32),
            VMEM((27 * PLANES, COLS), F32),
            VMEM((PLANES, COLS), F32),
        ),
        in_specs=[WHOLE] * 5,
        out_specs=(SOMEWHERE, WHOLE, WHOLE),
        input_output_aliases={0: 1, 1: 2},
        scratch_shapes=[pltpu.SemaphoreType.DMA((OUT_COPIES,))],
        compiler_params=params(16),
        name="finish",
    )(moved, bounce, x_other, dense, solid_mask.reshape(PLANES, COLS))
    return populations_next.reshape(populations.shape), (own + from_pair + from_other)[:3]


def solution(mesh):
    return jax.shard_map(
        per_device,
        mesh=mesh,
        in_specs=(
            P(None, None, "gx", "gy"),
            P(None, "gx", "gy"),
            P(("gx", "gy")),
            P(("gx", "gy")),
            P(("gx", "gy")),
            P(("gx", "gy")),
            P(("gx", "gy")),
        ),
        out_specs=(P(None, None, "gx", "gy"), P(None, ("gx", "gy"))),
        check_vma=False,
    )
```
